256 devices in a mesh: section: 16 (over y, z_hi), tp: 16 (over x, z_lo, core).
Axes of the slice: x: 4, y: 4, z: 8 (z_hi: 4, z_lo: 2; z = z_hi * 2 + z_lo), core: 2. Of those that a mesh axis runs over, the one named last changes fastest.
Arguments:
- saved_in: bfloat16 [16, 1024, 3072], P('section', 'tp'), may hold values from -6 to 6
- out_grad: bfloat16 [16, 1024, 3072], P('section', 'tp'), may hold values from -6 to 6
- pending: bfloat16 [16, 1024, 3072], P('section', 'tp'), may hold values from -6 to 6
- gain: float32 [16, 3072], P('section'), may hold values from 0.5 to 1.5
- alpha: float32 [16, 16], replicated, may hold values from 0.2 to 1
- w_query: bfloat16 [16, 3072, 4096], P('section', None, 'tp'), may hold values from -0.5 to 0.5
- w_key: bfloat16 [16, 3072, 4096], P('section', None, 'tp'), may hold values from -0.5 to 0.5
- w_value: bfloat16 [16, 3072, 4096], P('section', None, 'tp'), may hold values from -0.109375 to 0.109375
- w_out: bfloat16 [16, 4096, 3072], P('section', 'tp'), may hold values from -0.09375 to 0.09375
Outputs:
- in_grads: bfloat16 [16, 1024, 3072], P('section', 'tp')
- new_pending: bfloat16 [16, 1024, 3072], P('section', 'tp')
The draws below stay inside these ranges and needn't reach their ends.
All inputs are finite; a program needn't handle non-finite values.
Results may differ from the reference program's by a relative error of at most 0.029.
Values may be sent and summed in bfloat16 or wider, within the bound.
A program may use at most 256 MiB of HBM per device.

```python
import math
import jax
import jax.numpy as jnp
from jax import lax

D = 3072
HEAD = 128
TOKENS = 1024
HD = 4096
SECTIONS = 16


def draw_saved_in(key, part):
    own_key = jax.random.fold_in(key, 11)
    values = jnp.clip(jax.random.normal(own_key, (SECTIONS, TOKENS, D), jnp.float32), -6.0, 6.0)
    return values.astype(jnp.bfloat16)


def draw_w_query(key, part):
    own_key = jax.random.fold_in(key, 23)
    values = jnp.clip(jax.random.normal(own_key, (SECTIONS, D, HD), jnp.float32), -4.0, 4.0) * D ** (-0.5)
    return values.astype(jnp.bfloat16)


def draw_w_key(key, part):
    own_key = jax.random.fold_in(key, 37)
    values = jnp.clip(jax.random.normal(own_key, (SECTIONS, D, HD), jnp.float32), -4.0, 4.0) * D ** (-0.5)
    return values.astype(jnp.bfloat16)


def block_levels(rng, dims, pieces, low, largest):
    def one(position, blocks):
        steps = jax.random.uniform(jax.random.fold_in(jax.random.fold_in(rng, 6), position), (blocks,), jnp.float32, low / len(pieces), largest / len(pieces))
        return jnp.repeat(jnp.exp(steps), dims[position] // blocks).reshape((-1,) + (1,) * (len(dims) - position - 1))

    loudness = one(*pieces[0])
    for cut in pieces[1:]:
        loudness = loudness * one(*cut)
    return loudness


def scatter_about(key, dims, scale, limit, shards=(), held_as=jnp.bfloat16):
    array = scale * jax.random.normal(key, dims, jnp.float32)
    if shards:
        array = array * block_levels(key, dims, shards, -0.22, 0.18)
    return jnp.clip(array, -limit, limit).astype(held_as)


def setup_inputs(seed: int = 0) -> dict:
    seeds = jax.random.split(jax.random.key(seed), 10)
    return {
        "saved_in": draw_saved_in(jax.random.fold_in(seeds[9], 71), 0),
        "out_grad": scatter_about(seeds[1], (SECTIONS, TOKENS, D), 1.0, 6.0, ((0, 16), (1, 16))),
        "pending": scatter_about(seeds[2], (SECTIONS, TOKENS, D), 1.0, 6.0, ((0, 16), (1, 16))),
        "gain": jnp.clip(1.0 + 0.1 * jax.random.normal(seeds[3], (SECTIONS, D), jnp.float32), 0.5, 1.5),
        "alpha": jnp.clip(jax.random.uniform(seeds[4], (SECTIONS, SECTIONS), jnp.float32, 0.2, 1.0), 0.2, 1.0),
        "w_query": draw_w_query(jax.random.fold_in(seeds[9], 71), 0),
        "w_key": draw_w_key(jax.random.fold_in(seeds[9], 71), 0),
        "w_value": scatter_about(seeds[7], (SECTIONS, D, HD), D ** -0.5, 0.109375, ((0, 16), (2, 16))),
        "w_out": scatter_about(seeds[8], (SECTIONS, HD, D), HD ** -0.5, 0.09375, ((0, 16), (1, 16))),
    }


eps = 1e-05

def normalize(rows, gain_row):
    values = rows.astype(jnp.float32)
    factor = lax.rsqrt(lax.optimization_barrier(jnp.mean(values * values, axis=-1, keepdims=True)) + eps)
    return (values * factor * gain_row).astype(jnp.bfloat16)

def attend_back(query, keys, values, grad_heads):
    tokens = query.shape[0]
    heads = query.shape[1] // HEAD
    shape = (tokens, heads, HEAD)
    query = query.reshape(shape).astype(jnp.float32)
    keys = keys.reshape(shape).astype(jnp.float32)
    values = values.reshape(shape).astype(jnp.float32)
    grad_heads = grad_heads.reshape(shape).astype(jnp.float32)
    scale = 1.0 / math.sqrt(HEAD)
    scores = jnp.einsum('qhe,khe->hqk', query, keys) * scale
    causal = jnp.arange(tokens)[:, None] >= jnp.arange(tokens)[None, :]
    scores = jnp.where(causal[None], scores, -1e+30)
    peak = lax.optimization_barrier(jnp.max(scores, axis=-1, keepdims=True))
    weights = jnp.exp(scores - peak)
    weights = weights / lax.optimization_barrier(jnp.sum(weights, axis=-1, keepdims=True))
    probs = weights.astype(jnp.bfloat16).astype(jnp.float32)
    output = jnp.einsum('hqk,khe->hqe', probs, values)
    delta = jnp.einsum('qhe,hqe->hq', grad_heads, output)[:, :, None]
    grad_probs = jnp.einsum('qhe,khe->hqk', grad_heads, values)
    grad_scores = (weights * (grad_probs - delta) * scale).astype(jnp.bfloat16).astype(jnp.float32)
    grad_query = jnp.einsum('hqk,khe->qhe', grad_scores, keys).astype(jnp.bfloat16)
    grad_keys = jnp.einsum('hqk,qhe->khe', grad_scores, query).astype(jnp.bfloat16)
    grad_values = jnp.einsum('hqk,qhe->khe', probs, grad_heads).astype(jnp.bfloat16)
    flat = (tokens, heads * HEAD)
    return (grad_query.reshape(flat), grad_keys.reshape(flat), grad_values.reshape(flat))

def section_back(items):
    saved_rows, grad_rows, gain_row, query_weight, key_weight, value_weight, out_weight = items
    normed = normalize(saved_rows, gain_row)
    query = jnp.dot(normed, query_weight, preferred_element_type=jnp.float32).astype(jnp.bfloat16)
    keys = jnp.dot(normed, key_weight, preferred_element_type=jnp.float32).astype(jnp.bfloat16)
    values = jnp.dot(normed, value_weight, preferred_element_type=jnp.float32).astype(jnp.bfloat16)
    grad_heads = jnp.dot(grad_rows, out_weight.T, preferred_element_type=jnp.float32).astype(jnp.bfloat16)
    grad_query, grad_keys, grad_values = attend_back(query, keys, values, grad_heads)
    grad_normed = jnp.dot(grad_query, query_weight.T, preferred_element_type=jnp.float32)
    grad_normed = grad_normed + jnp.dot(grad_keys, key_weight.T, preferred_element_type=jnp.float32)
    grad_normed = grad_normed + jnp.dot(grad_values, value_weight.T, preferred_element_type=jnp.float32)
    saved_float = saved_rows.astype(jnp.float32)
    factor = lax.rsqrt(lax.optimization_barrier(jnp.mean(saved_float * saved_float, axis=-1, keepdims=True)) + eps)
    scaled = grad_normed * gain_row
    inner = lax.optimization_barrier(jnp.mean(scaled * saved_float, axis=-1, keepdims=True))
    result = grad_rows.astype(jnp.float32) + factor * (scaled - saved_float * factor * factor * inner)
    return result.astype(jnp.bfloat16)

def reference(saved_in, out_grad, pending, gain, alpha, w_query, w_key, w_value, w_out):
    sections = saved_in.shape[0]
    grads = lax.map(section_back, (saved_in, out_grad, gain, w_query, w_key, w_value, w_out))
    section_ids = jnp.arange(sections).astype(jnp.int32)

    def refresh(index):
        coeffs = jnp.where(section_ids > index, alpha[:, index], 0.0)

        def add_one(source, total):
            return total + coeffs[source] * grads[source].astype(jnp.float32)
        total = lax.fori_loop(0, sections, add_one, pending[index].astype(jnp.float32))
        return total.astype(jnp.bfloat16)
    updated = lax.map(refresh, section_ids)
    return (grads, updated)
```

```python
import functools
import math

import jax
import jax.numpy as jnp
from jax import lax
from jax.experimental import pallas as pl
from jax.experimental.pallas import tpu as pltpu
from jax.sharding import PartitionSpec as P

HEAD = 128
MESH = pl.DeviceIdType.MESH

eps = 1e-05


def normalize(rows, gain_row):
    values = rows.astype(jnp.float32)
    factor = lax.rsqrt(jnp.mean(values * values, axis=-1, keepdims=True) + eps)
    return (values * factor * gain_row).astype(jnp.bfloat16)


def project_rows(rows, gain_row, query_weight, key_weight, value_weight):
    normed = normalize(rows, gain_row)
    query = jnp.dot(normed, query_weight, preferred_element_type=jnp.float32).astype(jnp.bfloat16)
    keys = jnp.dot(normed, key_weight, preferred_element_type=jnp.float32).astype(jnp.bfloat16)
    values = jnp.dot(normed, value_weight, preferred_element_type=jnp.float32).astype(jnp.bfloat16)
    return query, keys, values


def heads_back(grad_rows, out_weight):
    product = jnp.einsum("td,ed->te", grad_rows, out_weight, preferred_element_type=jnp.float32)
    return product.astype(jnp.bfloat16)


def dot(a, b, ca, cb):
    return lax.dot_general(a, b, (((ca,), (cb,)), ((), ())), preferred_element_type=jnp.float32)


def attend_kernel(q_ref, k_ref, v_ref, g_ref, dq_ref, dk_ref, dv_ref, dk_acc, dv_acc, *, block):
    tokens, width = q_ref.shape
    scale = 1.0 / math.sqrt(HEAD)
    log2e = math.log2(math.e)
    below = lax.broadcasted_iota(jnp.int32, (block, block), 0) <= lax.broadcasted_iota(
        jnp.int32, (block, block), 1
    )
    for head in range(width // HEAD):
        cols = pl.ds(head * HEAD, HEAD)
        keys_t = k_ref[:, cols].T
        values_t = v_ref[:, cols].T
        for step in reversed(range(tokens // block)):
            n = (step + 1) * block
            rows = pl.ds(step * block, block)
            query, grad = q_ref[rows, cols], g_ref[rows, cols]
            scores = dot(k_ref[pl.ds(0, n), cols], query, 1, 1) * (scale * log2e)
            last = jnp.where(below, scores[n - block :], -1e30)
            scores = last if step == 0 else jnp.concatenate((scores[: n - block], last), axis=0)
            peak = jnp.max(scores, axis=0, keepdims=True)
            weights = jnp.exp2(scores - peak)
            weights = weights * (1.0 / jnp.sum(weights, axis=0, keepdims=True))
            probs = weights.astype(jnp.bfloat16)
            output_t = dot(values_t[:, :n], probs, 1, 0)
            grad_t = grad.astype(jnp.float32).T
            delta = jnp.sum(grad_t * output_t, axis=0, keepdims=True)
            grad_probs = dot(v_ref[pl.ds(0, n), cols], grad, 1, 1)
            grad_scores = (weights * ((grad_probs - delta) * scale)).astype(jnp.bfloat16)
            dq_ref[rows, cols] = dot(keys_t[:, :n], grad_scores, 1, 0).T.astype(jnp.bfloat16)
            more_k = dot(grad_scores, query, 1, 0)
            more_v = dot(probs, grad, 1, 0)
            if step == tokens // block - 1:
                dk_acc[...] = more_k
                dv_acc[...] = more_v
            else:
                dk_acc[pl.ds(0, n)] += more_k
                dv_acc[pl.ds(0, n)] += more_v
        dk_ref[:, cols] = dk_acc[...].astype(jnp.bfloat16)
        dv_ref[:, cols] = dv_acc[...].astype(jnp.bfloat16)


def attend_back(query, keys, values, grad_heads):
    tokens, width = query.shape
    out = jax.ShapeDtypeStruct((tokens, width), jnp.bfloat16)
    whole = pl.BlockSpec(memory_space=pltpu.VMEM)
    return pl.pallas_call(
        functools.partial(attend_kernel, block=256),
        out_shape=(out, out, out),
        in_specs=[whole] * 4,
        out_specs=(whole,) * 3,
        scratch_shapes=[pltpu.VMEM((tokens, HEAD), jnp.float32)] * 2,
        compiler_params=pltpu.CompilerParams(vmem_limit_bytes=40 * 2**20),
        cost_estimate=pl.CostEstimate(flops=2 * 10**9, bytes_accessed=4 * 10**6, transcendentals=10**6),
    )(query, keys, values, grad_heads)


def section_kernel(alpha_ref, mine_ref, pending_ref, out_ref, gather, part, stage, arrived,
                   send_sem, recv_sem, *, ny, nz):
    place = lax.axis_index("section")
    y, z = place // nz, lax.rem(place, nz)
    rows, depth = mine_ref.shape
    half, quarter = rows // 2, rows // 4
    wide = 512

    def at(dy, dz):
        return lax.rem(y + dy + ny, ny) * nz + lax.rem(z + dz + nz, nz)

    up = (at(1, 0), at(0, 1))
    down = (at(-1, 0), at(0, -1))

    barrier = pltpu.get_barrier_semaphore()
    for other in up + down:
        pl.semaphore_signal(barrier, inc=1, device_id={"section": other}, device_id_type=MESH)
    pl.semaphore_wait(barrier, 4)

    def copy(index, src, dst, to):
        return pltpu.make_async_remote_copy(
            src_ref=src, dst_ref=dst, send_sem=send_sem.at[index], recv_sem=recv_sem.at[index],
            device_id={"section": to}, device_id_type=MESH,
        )

    lo, hi = pl.ds(0, quarter), pl.ds(quarter, quarter)
    sends = []

    def go(c):
        c.start()
        sends.append(c)
        return c

    first = []
    for w in (1, 0):
        own = mine_ref.at[pl.ds(w * half, half)]
        first.append((
            w,
            go(copy(8 * w, own, gather.at[w, 1], up[w])),
            go(copy(8 * w + 1, own, gather.at[w, 3], down[w])),
        ))
    relay = {}
    for w in (0, 1):
        for which, a, b in first:
            if which == w:
                a.wait_recv()
                ra = go(copy(8 * w + 2, gather.at[w, 1, lo], gather.at[w, 2, lo], up[w]))
                b.wait_recv()
                rb = go(copy(8 * w + 3, gather.at[w, 3, hi], gather.at[w, 2, hi], down[w]))
                relay[w] = (ra, rb)
        if w == 0:
            pass

    def coefficient(j, s):
        return jnp.where(s > j, alpha_ref[s, j], 0.0)

    def combine(w, order):
        coeffs = {}
        for r in order:
            j = at(0, r) if w == 0 else at(r, 0)
            for t in range(4):
                s = at(-t, 0) if w == 0 else at(0, -t)
                coeffs[r, t] = coefficient(j, s)

        def body(i, carry):
            rr = pl.multiple_of(lax.rem(i, half // 16) * 16, 16)
            cc = pl.multiple_of((i // (half // 16)) * wide, wide)
            here, cols = pl.ds(rr, 16), pl.ds(cc, wide)
            blocks = [mine_ref[pl.ds(pl.multiple_of(w * half + rr, 16), 16), cols]]
            blocks += [gather[w, t, here, cols] for t in (1, 2, 3)]
            blocks = [b.astype(jnp.float32) for b in blocks]
            for r in order:
                total = blocks[0] * coeffs[r, 0]
                for t in (1, 2, 3):
                    total = total + blocks[t] * coeffs[r, t]
                part[w, r, here, cols] = total
                if r == 2:
                    stage[w, 2, here, cols] = total.astype(jnp.bfloat16)
            return carry

        lax.fori_loop(0, (half // 16) * (depth // wide), body, 0)

    def add_relay(w):
        def body(i, carry):
            cc = pl.multiple_of(i * wide, wide)
            cols = pl.ds(cc, wide)
            stage[w, 1, lo, cols] = (
                part[w, 1, lo, cols] + arrived[w, 2, lo, cols].astype(jnp.float32)
            ).astype(jnp.bfloat16)
            stage[w, 1, hi, cols] = part[w, 1, hi, cols].astype(jnp.bfloat16)
            stage[w, 3, lo, cols] = part[w, 3, lo, cols].astype(jnp.bfloat16)
            stage[w, 3, hi, cols] = (
                part[w, 3, hi, cols] + arrived[w, 2, hi, cols].astype(jnp.float32)
            ).astype(jnp.bfloat16)
            return carry

        lax.fori_loop(0, depth // wide, body, 0)

    def finish(w):
        def body(i, carry):
            rr = pl.multiple_of(lax.rem(i, half // 16) * 16, 16)
            cc = pl.multiple_of((i // (half // 16)) * wide, wide)
            here, cols = pl.ds(rr, 16), pl.ds(cc, wide)
            target = pl.ds(pl.multiple_of(w * half + rr, 16), 16)
            total = pending_ref[target, cols].astype(jnp.float32) + part[w, 0, here, cols]
            total = total + arrived[w, 1, here, cols].astype(jnp.float32)
            total = total + arrived[w, 3, here, cols].astype(jnp.float32)
            out_ref[target, cols] = total.astype(jnp.bfloat16)
            return carry

        lax.fori_loop(0, (half // 16) * (depth // wide), body, 0)

    second = {}
    for w in (0, 1):
        for c in relay[w]:
            c.wait_recv()
        combine(w, (0, 1, 2, 3))
        o = 1 - w
        second[w] = (
            go(copy(8 * w + 4, stage.at[w, 2, lo], arrived.at[w, 2, lo], up[o])),
            go(copy(8 * w + 5, stage.at[w, 2, hi], arrived.at[w, 2, hi], down[o])),
        )
    third = {}
    for w in (0, 1):
        for c in second[w]:
            c.wait_recv()
        add_relay(w)
        o = 1 - w
        third[w] = (
            go(copy(8 * w + 6, stage.at[w, 1], arrived.at[w, 1], up[o])),
            go(copy(8 * w + 7, stage.at[w, 3], arrived.at[w, 3], down[o])),
        )
    for w in (1, 0):
        for c in third[w]:
            c.wait_recv()
        finish(w)
    for c in sends:
        c.wait_send()


def section_sums(alpha, grad_input, pending):
    rows, depth = grad_input.shape
    half = rows // 2
    vmem = pl.BlockSpec(memory_space=pltpu.VMEM)
    return pl.pallas_call(
        functools.partial(section_kernel, ny=4, nz=4),
        out_shape=jax.ShapeDtypeStruct((rows, depth), jnp.bfloat16),
        in_specs=[pl.BlockSpec(memory_space=pltpu.SMEM), vmem, vmem],
        out_specs=vmem,
        scratch_shapes=[
            pltpu.VMEM((2, 4, half, depth), jnp.bfloat16),
            pltpu.VMEM((2, 4, half, depth), jnp.float32),
            pltpu.VMEM((2, 4, half, depth), jnp.bfloat16),
            pltpu.VMEM((2, 4, half, depth), jnp.bfloat16),
            pltpu.SemaphoreType.DMA((16,)),
            pltpu.SemaphoreType.DMA((16,)),
        ],
        compiler_params=pltpu.CompilerParams(
            collective_id=3, has_side_effects=True, vmem_limit_bytes=40 * 2**20
        ),
        cost_estimate=pl.CostEstimate(flops=10**7, bytes_accessed=10**6, transcendentals=0),
    )(alpha, grad_input, pending)


def on_device(saved_in, out_grad, pending, gain, alpha, w_query, w_key, w_value, w_out):
    saved_rows = saved_in[0]
    grad_rows = out_grad[0]
    gain_row = gain[0]
    query_weight = w_query[0]
    key_weight = w_key[0]
    value_weight = w_value[0]
    out_weight = w_out[0]
    all_saved, all_grads = (
        lax.all_gather(saved_rows, "tp", axis=0, tiled=True),
        lax.all_gather(grad_rows, "tp", axis=0, tiled=True),
    )
    query, keys, values = project_rows(all_saved, gain_row, query_weight, key_weight, value_weight)
    grad_heads = heads_back(all_grads, out_weight)
    grad_query, grad_keys, grad_values = attend_back(query, keys, values, grad_heads)
    rows = saved_rows.shape[0]
    total = jnp.zeros((lax.axis_size("tp") * rows, out_weight.shape[1]), jnp.float32)
    for grad_part, weight in (
        (grad_query, query_weight),
        (grad_keys, key_weight),
        (grad_values, value_weight),
    ):
        total = total + jnp.einsum(
            "te,de->td", grad_part, weight, preferred_element_type=jnp.float32
        )
    grad_normed = lax.psum_scatter(
        total.astype(jnp.bfloat16), "tp", scatter_dimension=0, tiled=True
    ).astype(jnp.float32)
    saved_float = saved_rows.astype(jnp.float32)
    factor = lax.rsqrt(jnp.mean(saved_float * saved_float, axis=-1, keepdims=True) + eps)
    scaled = grad_normed * gain_row
    inner = jnp.mean(scaled * saved_float, axis=-1, keepdims=True)
    grad_input = (
        grad_rows.astype(jnp.float32) + factor * (scaled - saved_float * factor * factor * inner)
    ).astype(jnp.bfloat16)
    updated = section_sums(alpha, grad_input, pending[0])
    return (grad_input[None], updated[None])


def solution(mesh):
    return jax.shard_map(
        on_device,
        mesh=mesh,
        in_specs=(
            P("section", "tp", None),
            P("section", "tp", None),
            P("section", "tp", None),
            P("section", None),
            P(),
            P("section", None, "tp"),
            P("section", None, "tp"),
            P("section", None, "tp"),
            P("section", "tp", None),
        ),
        out_specs=(P("section", "tp", None), P("section", "tp", None)),
        check_vma=False,
    )
```

```python
import functools
import math

import jax
import jax.numpy as jnp
from jax import lax
from jax.experimental import pallas as pl
from jax.experimental.pallas import tpu as pltpu
from jax.sharding import PartitionSpec as P

HEAD = 128
MESH = pl.DeviceIdType.MESH

eps = 1e-05


def dot(a, b, ca, cb):
    return lax.dot_general(a, b, (((ca,), (cb,)), ((), ())), preferred_element_type=jnp.float32)


def attend_kernel(in_ref, out_ref, q_ref, k_ref, v_ref, g_ref, dk_acc, dv_acc, *, block, rows):
    tokens, width = q_ref.shape
    scale = 1.0 / math.sqrt(HEAD)
    log2e = math.log2(math.e)
    places = [(chip, core, pl.ds((2 * chip + core) * rows, rows))
              for chip in range(tokens // (2 * rows)) for core in (0, 1)]
    for j, ref in enumerate((q_ref, k_ref, v_ref, g_ref)):
        for chip, core, here in places:
            ref[here, :] = in_ref[core, j, pl.ds(chip * rows, rows), :]
    below = lax.broadcasted_iota(jnp.int32, (block, block), 0) <= lax.broadcasted_iota(
        jnp.int32, (block, block), 1
    )
    for head in range(width // HEAD):
        cols = pl.ds(head * HEAD, HEAD)
        keys_t = k_ref[:, cols].T
        values_t = v_ref[:, cols].T
        for step in reversed(range(tokens // block)):
            n = (step + 1) * block
            mine = pl.ds(step * block, block)
            query, grad = q_ref[mine, cols], g_ref[mine, cols]
            scores = dot(k_ref[pl.ds(0, n), cols], query, 1, 1) * (scale * log2e)
            last = jnp.where(below, scores[n - block :], -1e30)
            scores = last if step == 0 else jnp.concatenate((scores[: n - block], last), axis=0)
            peak = jnp.max(scores, axis=0, keepdims=True)
            weights = jnp.exp2(scores - peak)
            weights = weights * (1.0 / jnp.sum(weights, axis=0, keepdims=True))
            probs = weights.astype(jnp.bfloat16)
            output_t = dot(values_t[:, :n], probs, 1, 0)
            grad_t = grad.astype(jnp.float32).T
            delta = jnp.sum(grad_t * output_t, axis=0, keepdims=True)
            grad_probs = dot(v_ref[pl.ds(0, n), cols], grad, 1, 1)
            grad_scores = (weights * ((grad_probs - delta) * scale)).astype(jnp.bfloat16)
            grad_query = dot(keys_t[:, :n], grad_scores, 1, 0).T.astype(jnp.bfloat16)
            for chip, core, here in places:
                offset = (2 * chip + core) * rows - step * block
                if 0 <= offset < block:
                    out_ref[core, 0, pl.ds(chip * rows, rows), cols] = grad_query[offset : offset + rows]
            more_k = dot(grad_scores, query, 1, 0)
            more_v = dot(probs, grad, 1, 0)
            if step == tokens // block - 1:
                dk_acc[...] = more_k
                dv_acc[...] = more_v
            else:
                dk_acc[pl.ds(0, n)] += more_k
                dv_acc[pl.ds(0, n)] += more_v
        for j, acc in ((1, dk_acc), (2, dv_acc)):
            for chip, core, here in places:
                out_ref[core, j, pl.ds(chip * rows, rows), cols] = acc[here, :].astype(jnp.bfloat16)


def attend_back(heads, rows):
    _, _, half, width = heads.shape
    tokens = 2 * half
    whole = pl.BlockSpec(memory_space=pltpu.VMEM)
    return pl.pallas_call(
        functools.partial(attend_kernel, block=256, rows=rows),
        out_shape=jax.ShapeDtypeStruct((2, 3, half, width), jnp.bfloat16),
        in_specs=[whole],
        out_specs=whole,
        scratch_shapes=[pltpu.VMEM((tokens, width), jnp.bfloat16)] * 4
        + [pltpu.VMEM((tokens, HEAD), jnp.float32)] * 2,
        compiler_params=pltpu.CompilerParams(vmem_limit_bytes=40 * 2**20),
        cost_estimate=pl.CostEstimate(flops=2 * 10**9, bytes_accessed=4 * 10**6, transcendentals=10**6),
    )(heads)


def tile_loop(rows, depth, wide, body):
    tall = rows // 16

    def step(i, carry):
        rr = pl.multiple_of(lax.rem(i, tall) * 16, 16)
        cc = pl.multiple_of((i // tall) * wide, wide)
        body(pl.ds(rr, 16), pl.ds(cc, wide))
        return carry

    lax.fori_loop(0, tall * (depth // wide), step, 0)


def greet(others):
    barrier = pltpu.get_barrier_semaphore()
    for other in others:
        pl.semaphore_signal(barrier, inc=1, device_id={"tp": other}, device_id_type=MESH)
    pl.semaphore_wait(barrier, len(others))


def neighbours():
    place = lax.axis_index("tp")
    x, z, core = place // 4, lax.rem(place // 2, 2), lax.rem(place, 2)
    right = lax.rem(x + 1, 4) * 4 + z * 2 + core
    left = lax.rem(x + 3, 4) * 4 + z * 2 + core
    across = x * 4 + (1 - z) * 2 + core
    twin = x * 4 + z * 2 + (1 - core)
    return x, z, core, right, left, across, twin


def project_kernel(saved_ref, grad_ref, gain_ref, wq_ref, wk_ref, wv_ref, wo_ref, heads_ref, twin_ref,
                   normed, grads, weights, out_weights, theirs, send_sem, recv_sem, load_sem, store_sem):
    x, z, core, right, left, across, twin = neighbours()
    rows, depth = saved_ref.shape
    width = wq_ref.shape[1]
    pair = 2 * rows
    half = rows // 2
    lo, hi = pl.ds(0, half), pl.ds(half, half)
    other = 1 - z
    sends = []

    loads = [
        pltpu.make_async_copy(wq_ref, weights.at[0, 0], load_sem.at[0]),
        pltpu.make_async_copy(wk_ref, weights.at[0, 1], load_sem.at[1]),
        pltpu.make_async_copy(wv_ref, weights.at[0, 2], load_sem.at[2]),
        pltpu.make_async_copy(wo_ref, out_weights.at[0], load_sem.at[3]),
    ]
    greet((right, left, across, twin))

    def go(index, src, dst, to):
        c = pltpu.make_async_remote_copy(
            src_ref=src, dst_ref=dst, send_sem=send_sem.at[index], recv_sem=recv_sem.at[index],
            device_id={"tp": to}, device_id_type=MESH,
        )
        c.start()
        sends.append(c)
        return c

    g_right = go(0, grad_ref, grads.at[1, z], right)
    g_left = go(1, grad_ref, grads.at[3, z], left)

    def norm(i, carry):
        here = pl.ds(pl.multiple_of(i * 16, 16), 16)
        values = saved_ref[here, :].astype(jnp.float32)
        factor = lax.rsqrt(jnp.mean(values * values, axis=-1, keepdims=True) + eps)
        normed[0, z, here, :] = (values * factor * gain_ref[...]).astype(jnp.bfloat16)
        return carry

    lax.fori_loop(0, rows // 16, norm, 0)
    n_across = go(8, normed.at[0, z], normed.at[0, z], across)
    n_right = go(9, normed.at[0, z], normed.at[1, z], right)
    n_left = go(10, normed.at[0, z], normed.at[3, z], left)
    g_across = go(4, grad_ref, grads.at[0, z], across)
    for c in loads:
        c.start()
    w_twin = [
        go(17, wq_ref, weights.at[1, 0], twin),
        go(18, wk_ref, weights.at[1, 1], twin),
        go(19, wv_ref, weights.at[1, 2], twin),
        go(20, wo_ref, out_weights.at[1], twin),
    ]
    grads[0, z] = grad_ref[...]

    def place_of(r):
        return pl.ds(pl.multiple_of(lax.rem(x + 4 - r, 4) * pair, pair), pair)

    def project(r, which):
        here = place_of(r)

        def one(j, carry):
            block = normed[r].reshape(pair, depth)
            result = dot(block, weights[which, j], 1, 0).astype(jnp.bfloat16)
            if which == 0:
                heads_ref[core, j, here, :] = result
            else:
                theirs[j, here, :] = result
            return carry

        lax.fori_loop(0, 3, one, 0)

    def project_grads(r, which):
        here = place_of(r)
        result = dot(grads[r].reshape(pair, depth), out_weights[which], 1, 1).astype(jnp.bfloat16)
        if which == 0:
            heads_ref[core, 3, here, :] = result
        else:
            theirs[3, here, :] = result

    results = []

    def hand_over(index, r, first, count):
        js, here = pl.ds(first, count), place_of(r)
        results.append(go(index, theirs.at[js, here], heads_ref.at[core, js, here], twin))

    n_across.wait_recv()
    no_right = go(11, normed.at[0, other], normed.at[1, other], right)
    no_left = go(12, normed.at[0, other], normed.at[3, other], left)
    for c in loads[:3]:
        c.wait()
    project(0, 0)
    g_right.wait_recv()
    g_relay_right = go(2, grads.at[1, z, lo], grads.at[2, z, lo], right)
    g_one = go(5, grads.at[1, z], grads.at[1, z], across)
    g_left.wait_recv()
    g_relay_left = go(3, grads.at[3, z, hi], grads.at[2, z, hi], left)
    g_three = go(6, grads.at[3, z], grads.at[3, z], across)
    loads[3].wait()
    n_right.wait_recv()
    n_relay_right = go(13, normed.at[1, z, lo], normed.at[2, z, lo], right)
    n_left.wait_recv()
    n_relay_left = go(14, normed.at[3, z, hi], normed.at[2, z, hi], left)
    g_relay_right.wait_recv()
    g_relay_left.wait_recv()
    g_two = go(7, grads.at[2, z], grads.at[2, z], across)
    g_across.wait_recv()
    project_grads(0, 0)
    no_right.wait_recv()
    no_relay_right = go(15, normed.at[1, other, lo], normed.at[2, other, lo], right)
    no_left.wait_recv()
    no_relay_left = go(16, normed.at[3, other, hi], normed.at[2, other, hi], left)
    project(1, 0)
    project(3, 0)
    for c in w_twin:
        c.wait_recv()
    stores = [
        pltpu.make_async_copy(weights.at[1, j], twin_ref.at[j], store_sem.at[j]) for j in range(3)
    ]
    for c in stores:
        c.start()
    for index, r in ((21, 0), (22, 1), (23, 3)):
        project(r, 1)
        hand_over(index, r, 0, 3)
    project_grads(0, 1)
    hand_over(25, 0, 3, 1)
    for index, r, c in ((26, 1, g_one), (27, 3, g_three)):
        c.wait_recv()
        project_grads(r, 1)
        hand_over(index, r, 3, 1)
        project_grads(r, 0)
    for c in (n_relay_right, n_relay_left, no_relay_right, no_relay_left):
        c.wait_recv()
    project(2, 1)
    hand_over(24, 2, 0, 3)
    project(2, 0)
    g_two.wait_recv()
    project_grads(2, 1)
    hand_over(28, 2, 3, 1)
    project_grads(2, 0)
    for c in results:
        c.wait_recv()
    for c in sends:
        c.wait_send()
    for c in stores:
        c.wait()


def project_all(saved, grad, gain, wq, wk, wv, wo):
    rows, depth = saved.shape
    width = wq.shape[1]
    vmem = pl.BlockSpec(memory_space=pltpu.VMEM)
    hbm = pl.BlockSpec(memory_space=pl.ANY)
    return pl.pallas_call(
        project_kernel,
        out_shape=(
            jax.ShapeDtypeStruct((2, 4, 8 * rows, width), jnp.bfloat16),
            jax.ShapeDtypeStruct((3, depth, width), jnp.bfloat16),
        ),
        in_specs=[vmem, vmem, vmem, hbm, hbm, hbm, hbm],
        out_specs=(vmem, hbm),
        scratch_shapes=[
            pltpu.VMEM((4, 2, rows, depth), jnp.bfloat16),
            pltpu.VMEM((4, 2, rows, depth), jnp.bfloat16),
            pltpu.VMEM((2, 3, depth, width), jnp.bfloat16),
            pltpu.VMEM((2, width, depth), jnp.bfloat16),
            pltpu.VMEM((4, 8 * rows, width), jnp.bfloat16),
            pltpu.SemaphoreType.DMA((29,)),
            pltpu.SemaphoreType.DMA((29,)),
            pltpu.SemaphoreType.DMA((4,)),
            pltpu.SemaphoreType.DMA((3,)),
        ],
        compiler_params=pltpu.CompilerParams(
            collective_id=1, has_side_effects=True, vmem_limit_bytes=56 * 2**20
        ),
        cost_estimate=pl.CostEstimate(flops=6 * 10**9, bytes_accessed=10**7, transcendentals=0),
    )(saved, grad, gain, wq, wk, wv, wo)


def input_kernel(d_ref, wq_ref, wk_ref, wv_ref, twin_ref, saved_ref, grad_ref, gain_ref, out_ref,
                 weights, theirs, part, za, xa1, xa2, xb1, xb2, zb, summed, send_sem, recv_sem, load_sem):
    x, z, core, right, left, across, twin = neighbours()
    rows, depth = saved_ref.shape
    wide = part.shape[4]
    pair = 2 * rows
    lo, hi = pl.ds(0, rows // 2), pl.ds(rows // 2, rows // 2)
    other = 1 - z
    chunk = 512
    chunks = depth // chunk
    f32 = jnp.float32
    sends = []

    loads = []
    for n in range(chunks):
        here = pl.ds(n * chunk, chunk)
        sources = [w.at[here] for w in (wq_ref, wk_ref, wv_ref)] + [twin_ref.at[j, here] for j in range(3)]
        loads.append([
            pltpu.make_async_copy(s, weights.at[j, here], load_sem.at[n, j]) for j, s in enumerate(sources)
        ])
    for n in range(chunks):
        for c in loads[n]:
            c.start()
    greet((right, left, across, twin))

    def go(index, src, dst, to):
        c = pltpu.make_async_remote_copy(
            src_ref=src, dst_ref=dst, send_sem=send_sem.at[index], recv_sem=recv_sem.at[index],
            device_id={"tp": to}, device_id_type=MESH,
        )
        c.start()
        sends.append(c)
        return c

    swap = go(0, d_ref.at[1 - core], theirs, twin)

    def one_chunk(r, n):
        here = pl.ds(pl.multiple_of(lax.rem(x + r, 4) * pair, pair), pair)
        cols = pl.ds(pl.multiple_of(n * chunk, chunk), chunk)
        total = dot(d_ref[core, 0, here, :], weights[0, cols, :], 1, 1)
        for j in (1, 2):
            total += dot(d_ref[core, j, here, :], weights[j, cols, :], 1, 1)
        for j in (0, 1, 2):
            total += dot(theirs[j, here, :], weights[3 + j, cols, :], 1, 1)
        per = wide // chunk
        into = pl.ds(pl.multiple_of(lax.rem(n, per) * chunk, chunk), chunk)
        part[r, :, n // per, :, into] = total.astype(jnp.bfloat16).reshape(2, rows, chunk)

    def block(r):
        def step(n, carry):
            one_chunk(r, n)
            return carry

        lax.fori_loop(0, chunks, step, 0)

    def add(target, source, count):
        def body(here, cols):
            target[here, cols] = (
                target[here, cols].astype(f32) + source[here, cols].astype(f32)
            ).astype(jnp.bfloat16)

        tile_loop(count, wide, chunk, body)

    swap.wait_recv()
    for n in range(chunks):
        for c in loads[n]:
            c.wait()
        one_chunk(2, n)
    xb1_right = go(1, part.at[2, 0, 1], xb1.at[0], right)
    xb1_left = go(2, part.at[2, 1, 1], xb1.at[1], left)
    za_two = go(3, part.at[2, other, 0], za.at[2], across)
    block(1)
    xb2_right = [None, go(4, part.at[1, 1, 1], xb2.at[0, 1], right)]
    za_one = go(5, part.at[1, other, 0], za.at[1], across)
    block(3)
    xb2_left = [go(6, part.at[3, 0, 1], xb2.at[1, 0], left), None]
    za_three = go(7, part.at[3, other, 0], za.at[3], across)
    xb1_right.wait_recv()
    add(part.at[1, 0, 1], xb1.at[0], rows)
    xb2_right[0] = go(8, part.at[1, 0, 1], xb2.at[0, 0], right)
    xb1_left.wait_recv()
    add(part.at[3, 1, 1], xb1.at[1], rows)
    xb2_left[1] = go(9, part.at[3, 1, 1], xb2.at[1, 1], left)
    za_two.wait_recv()
    add(part.at[2, z, 0], za.at[2], rows)
    xa1_right = go(10, part.at[2, z, 0, lo], xa1.at[lo], right)
    xa1_left = go(11, part.at[2, z, 0, hi], xa1.at[hi], left)
    block(0)
    za_zero = go(12, part.at[0, other, 0], za.at[0], across)
    za_one.wait_recv()
    add(part.at[1, z, 0], za.at[1], rows)
    xa1_right.wait_recv()
    add(part.at[1, z, 0, lo], xa1.at[lo], rows // 2)
    xa2_right = go(13, part.at[1, z, 0], xa2.at[0], right)
    za_three.wait_recv()
    add(part.at[3, z, 0], za.at[3], rows)
    xa1_left.wait_recv()
    add(part.at[3, z, 0, hi], xa1.at[hi], rows // 2)
    xa2_left = go(14, part.at[3, z, 0], xa2.at[1], left)
    for c in xb2_right + xb2_left:
        c.wait_recv()

    def fold(here, cols):
        total = part[0, other, 1, here, cols].astype(f32) + xb2[0, other, here, cols].astype(f32)
        part[0, other, 1, here, cols] = (total + xb2[1, other, here, cols].astype(f32)).astype(jnp.bfloat16)

    tile_loop(rows, wide, chunk, fold)
    zb_across = go(15, part.at[0, other, 1], zb, across)

    def fold_own(here, cols):
        total = part[0, z, 1, here, cols].astype(f32) + xb2[0, z, here, cols].astype(f32)
        summed[1, here, cols] = total + xb2[1, z, here, cols].astype(f32)

    tile_loop(rows, wide, chunk, fold_own)
    za_zero.wait_recv()
    xa2_right.wait_recv()
    xa2_left.wait_recv()

    def fold_first(here, cols):
        total = part[0, z, 0, here, cols].astype(f32) + za[0, here, cols].astype(f32)
        total = total + xa2[0, here, cols].astype(f32)
        summed[0, here, cols] = total + xa2[1, here, cols].astype(f32)

    tile_loop(rows, wide, chunk, fold_first)
    zb_across.wait_recv()

    def norm_back(i, carry):
        here = pl.ds(pl.multiple_of(i * 16, 16), 16)
        values = saved_ref[here, :].astype(f32)
        factor = lax.rsqrt(jnp.mean(values * values, axis=-1, keepdims=True) + eps)
        inner = jnp.zeros((16, 1), f32)
        for h in (0, 1):
            cols = pl.ds(h * wide, wide)
            scaled = summed[h, here, :]
            if h == 1:
                scaled = scaled + zb[here, :].astype(f32)
            scaled = scaled * gain_ref[:, cols]
            summed[h, here, :] = scaled
            inner = inner + jnp.sum(scaled * saved_ref[here, cols].astype(f32), axis=-1, keepdims=True)
        inner = inner * (1.0 / depth) * factor * factor
        for h in (0, 1):
            cols = pl.ds(h * wide, wide)
            term = summed[h, here, :] - saved_ref[here, cols].astype(f32) * inner
            out_ref[here, cols] = (grad_ref[here, cols].astype(f32) + factor * term).astype(jnp.bfloat16)
        return carry

    lax.fori_loop(0, rows // 16, norm_back, 0)
    for c in sends:
        c.wait_send()


def input_grads(d, wq, wk, wv, twin, saved, grad, gain):
    rows, depth = saved.shape
    width = wq.shape[1]
    wide = depth // 2
    vmem = pl.BlockSpec(memory_space=pltpu.VMEM)
    hbm = pl.BlockSpec(memory_space=pl.ANY)
    bf16 = jnp.bfloat16
    return pl.pallas_call(
        input_kernel,
        out_shape=jax.ShapeDtypeStruct((rows, depth), bf16),
        in_specs=[vmem, hbm, hbm, hbm, hbm, vmem, vmem, vmem],
        out_specs=vmem,
        scratch_shapes=[
            pltpu.VMEM((6, depth, width), bf16),
            pltpu.VMEM((3, 8 * rows, width), bf16),
            pltpu.VMEM((4, 2, 2, rows, wide), bf16),
            pltpu.VMEM((4, rows, wide), bf16),
            pltpu.VMEM((rows, wide), bf16),
            pltpu.VMEM((2, rows, wide), bf16),
            pltpu.VMEM((2, rows, wide), bf16),
            pltpu.VMEM((2, 2, rows, wide), bf16),
            pltpu.VMEM((rows, wide), bf16),
            pltpu.VMEM((2, rows, wide), jnp.float32),
            pltpu.SemaphoreType.DMA((16,)),
            pltpu.SemaphoreType.DMA((16,)),
            pltpu.SemaphoreType.DMA((depth // 512, 6)),
        ],
        compiler_params=pltpu.CompilerParams(
            collective_id=2, has_side_effects=True, vmem_limit_bytes=56 * 2**20
        ),
        cost_estimate=pl.CostEstimate(flops=5 * 10**9, bytes_accessed=10**7, transcendentals=0),
    )(d, wq, wk, wv, twin, saved, grad, gain)


def section_kernel(alpha_ref, mine_ref, pending_ref, out_ref, gather, part, stage, arrived,
                   send_sem, recv_sem, *, ny, nz):
    place = lax.axis_index("section")
    y, z = place // nz, lax.rem(place, nz)
    rows, depth = mine_ref.shape
    half, quarter = rows // 2, rows // 4
    wide = 512

    def at(dy, dz):
        return lax.rem(y + dy + ny, ny) * nz + lax.rem(z + dz + nz, nz)

    up = (at(1, 0), at(0, 1))
    down = (at(-1, 0), at(0, -1))

    barrier = pltpu.get_barrier_semaphore()
    for other in up + down:
        pl.semaphore_signal(barrier, inc=1, device_id={"section": other}, device_id_type=MESH)
    pl.semaphore_wait(barrier, 4)

    def copy(index, src, dst, to):
        return pltpu.make_async_remote_copy(
            src_ref=src, dst_ref=dst, send_sem=send_sem.at[index], recv_sem=recv_sem.at[index],
            device_id={"section": to}, device_id_type=MESH,
        )

    lo, hi = pl.ds(0, quarter), pl.ds(quarter, quarter)
    sends = []

    def go(c):
        c.start()
        sends.append(c)
        return c

    first = []
    for w in (1, 0):
        own = mine_ref.at[pl.ds(w * half, half)]
        first.append((
            w,
            go(copy(8 * w, own, gather.at[w, 1], up[w])),
            go(copy(8 * w + 1, own, gather.at[w, 3], down[w])),
        ))
    relay = {}
    for w in (0, 1):
        for which, a, b in first:
            if which == w:
                a.wait_recv()
                ra = go(copy(8 * w + 2, gather.at[w, 1, lo], gather.at[w, 2, lo], up[w]))
                b.wait_recv()
                rb = go(copy(8 * w + 3, gather.at[w, 3, hi], gather.at[w, 2, hi], down[w]))
                relay[w] = (ra, rb)
        if w == 0:
            pass

    def coefficient(j, s):
        return jnp.where(s > j, alpha_ref[s, j], 0.0)

    def combine(w, order):
        coeffs = {}
        for r in order:
            j = at(0, r) if w == 0 else at(r, 0)
            for t in range(4):
                s = at(-t, 0) if w == 0 else at(0, -t)
                coeffs[r, t] = coefficient(j, s)

        def body(i, carry):
            rr = pl.multiple_of(lax.rem(i, half // 16) * 16, 16)
            cc = pl.multiple_of((i // (half // 16)) * wide, wide)
            here, cols = pl.ds(rr, 16), pl.ds(cc, wide)
            blocks = [mine_ref[pl.ds(pl.multiple_of(w * half + rr, 16), 16), cols]]
            blocks += [gather[w, t, here, cols] for t in (1, 2, 3)]
            blocks = [b.astype(jnp.float32) for b in blocks]
            for r in order:
                total = blocks[0] * coeffs[r, 0]
                for t in (1, 2, 3):
                    total = total + blocks[t] * coeffs[r, t]
                part[w, r, here, cols] = total
                if r == 2:
                    stage[w, 2, here, cols] = total.astype(jnp.bfloat16)
            return carry

        lax.fori_loop(0, (half // 16) * (depth // wide), body, 0)

    def add_relay(w):
        def body(i, carry):
            cc = pl.multiple_of(i * wide, wide)
            cols = pl.ds(cc, wide)
            stage[w, 1, lo, cols] = (
                part[w, 1, lo, cols] + arrived[w, 2, lo, cols].astype(jnp.float32)
            ).astype(jnp.bfloat16)
            stage[w, 1, hi, cols] = part[w, 1, hi, cols].astype(jnp.bfloat16)
            stage[w, 3, lo, cols] = part[w, 3, lo, cols].astype(jnp.bfloat16)
            stage[w, 3, hi, cols] = (
                part[w, 3, hi, cols] + arrived[w, 2, hi, cols].astype(jnp.float32)
            ).astype(jnp.bfloat16)
            return carry

        lax.fori_loop(0, depth // wide, body, 0)

    def finish(w):
        def body(i, carry):
            rr = pl.multiple_of(lax.rem(i, half // 16) * 16, 16)
            cc = pl.multiple_of((i // (half // 16)) * wide, wide)
            here, cols = pl.ds(rr, 16), pl.ds(cc, wide)
            target = pl.ds(pl.multiple_of(w * half + rr, 16), 16)
            total = pending_ref[target, cols].astype(jnp.float32) + part[w, 0, here, cols]
            total = total + arrived[w, 1, here, cols].astype(jnp.float32)
            total = total + arrived[w, 3, here, cols].astype(jnp.float32)
            out_ref[target, cols] = total.astype(jnp.bfloat16)
            return carry

        lax.fori_loop(0, (half // 16) * (depth // wide), body, 0)

    second = {}
    for w in (0, 1):
        for c in relay[w]:
            c.wait_recv()
        combine(w, (0, 1, 2, 3))
        o = 1 - w
        second[w] = (
            go(copy(8 * w + 4, stage.at[w, 2, lo], arrived.at[w, 2, lo], up[o])),
            go(copy(8 * w + 5, stage.at[w, 2, hi], arrived.at[w, 2, hi], down[o])),
        )
    third = {}
    for w in (0, 1):
        for c in second[w]:
            c.wait_recv()
        add_relay(w)
        o = 1 - w
        third[w] = (
            go(copy(8 * w + 6, stage.at[w, 1], arrived.at[w, 1], up[o])),
            go(copy(8 * w + 7, stage.at[w, 3], arrived.at[w, 3], down[o])),
        )
    for w in (1, 0):
        for c in third[w]:
            c.wait_recv()
        finish(w)
    for c in sends:
        c.wait_send()


def section_sums(alpha, grad_input, pending):
    rows, depth = grad_input.shape
    half = rows // 2
    vmem = pl.BlockSpec(memory_space=pltpu.VMEM)
    return pl.pallas_call(
        functools.partial(section_kernel, ny=4, nz=4),
        out_shape=jax.ShapeDtypeStruct((rows, depth), jnp.bfloat16),
        in_specs=[pl.BlockSpec(memory_space=pltpu.SMEM), vmem, vmem],
        out_specs=vmem,
        scratch_shapes=[
            pltpu.VMEM((2, 4, half, depth), jnp.bfloat16),
            pltpu.VMEM((2, 4, half, depth), jnp.float32),
            pltpu.VMEM((2, 4, half, depth), jnp.bfloat16),
            pltpu.VMEM((2, 4, half, depth), jnp.bfloat16),
            pltpu.SemaphoreType.DMA((16,)),
            pltpu.SemaphoreType.DMA((16,)),
        ],
        compiler_params=pltpu.CompilerParams(
            collective_id=3, has_side_effects=True, vmem_limit_bytes=40 * 2**20
        ),
        cost_estimate=pl.CostEstimate(flops=10**7, bytes_accessed=10**6, transcendentals=0),
    )(alpha, grad_input, pending)


def on_device(saved_in, out_grad, pending, gain, alpha, w_query, w_key, w_value, w_out):
    saved, grad = saved_in[0], out_grad[0]
    wq, wk, wv, wo = w_query[0], w_key[0], w_value[0], w_out[0]
    heads, twin = project_all(saved, grad, gain, wq, wk, wv, wo)
    back = attend_back(heads, saved.shape[0])
    grad_input = input_grads(back, wq, wk, wv, twin, saved, grad, gain)
    updated = section_sums(alpha, grad_input, pending[0])
    return (grad_input[None], updated[None])


def solution(mesh):
    return jax.shard_map(
        on_device,
        mesh=mesh,
        in_specs=(
            P("section", "tp", None),
            P("section", "tp", None),
            P("section", "tp", None),
            P("section", None),
            P(),
            P("section", None, "tp"),
            P("section", None, "tp"),
            P("section", None, "tp"),
            P("section", "tp", None),
        ),
        out_specs=(P("section", "tp", None), P("section", "tp", None)),
        check_vma=False,
    )
```

```python
import math

import jax
import jax.numpy as jnp
from jax import lax
from jax.experimental import pallas as pl
from jax.experimental.pallas import tpu as pltpu
from jax.sharding import PartitionSpec as P

HEAD = 128
SLAB = 16
MESH = pl.DeviceIdType.MESH

eps = 1e-05

f32, bf16 = jnp.float32, jnp.bfloat16

GATHER = (
    "gLlo", "gRlo", "gA", "nrm", "nRhi", "gLhi", "nLlo", "gxR", "nLhi", "nA", "nRlo", "gxL", "gRhi",
    "g3A", "oRlo", "oLhi", "P0t", "P0", "oRhi", "oLlo", "g1A", "G0", "G3", "oxL", "nxR", "oxR",
    "P1t", "g2Ahi", "P3t", "nxL", "P3", "P1", "g2Alo", "G1", "zxR", "zxL", "P2t", "P2", "G2",
)
SUMS = (
    "product0", "first0", "product2", "first1", "second0", "second1", "across0", "first2", "norm0",
    "first3", "across1", "relay_y0", "second2", "relay_z0", "sums_y0", "norm1", "second3",
    "across2", "relay_y1", "relay_z1", "across3", "norm2", "sums_y1", "relay_y2", "sums_y2",
    "norm3", "sums_z0", "sums_z1", "relay_y3", "relay_z2", "late_y2", "relay_z3", "late_z0",
    "sums_y3", "sums_z2", "late_y0", "sums_z3", "late_y1", "late_z2", "late_y3", "late_z1",
    "late_z3", "finish0", "finish2", "finish1", "finish3",
)

def dot(a, b, ca, cb):
    return lax.dot_general(a, b, (((ca,), (cb,)), ((), ())), preferred_element_type=f32)


def neighbours():
    place = lax.axis_index("tp")
    x, z, core = place // 4, lax.rem(place // 2, 2), lax.rem(place, 2)
    right = lax.rem(x + 1, 4) * 4 + z * 2 + core
    left = lax.rem(x + 3, 4) * 4 + z * 2 + core
    across = x * 4 + (1 - z) * 2 + core
    twin = x * 4 + z * 2 + (1 - core)
    return x, z, core, {"tp": right}, {"tp": left}, {"tp": across}, {"tp": twin}


def kernel(alpha_ref, saved_ref, gain_ref, grad_ref, pending_ref, wq_ref, wk_ref, wv_ref, wo_ref,
           in_grads_ref, updated_ref,
           normed, grads, weights, out_weights, theirs, heads,
           q_ref, k_ref, v_ref, g_ref, dk_acc, dv_acc,
           back, back_twin, part, xb1, xb2, zb,
           pending, gather, stage, arrived, kept,
           send_sem, recv_sem, load_sem):
    x, z, core, right, left, across, twin = neighbours()
    section = lax.axis_index("section")
    y, zh = section // 4, lax.rem(section, 4)
    rows, depth = saved_ref.shape
    width = wq_ref.shape[1]
    pair, half = 2 * rows, rows // 2
    wide = depth // 2
    narrow = wide // 2
    other = 1 - z

    def at(dy, dz):
        return lax.rem(y + dy + 4, 4) * 4 + lax.rem(zh + dz + 4, 4)

    up = ({"section": at(1, 0)}, {"section": at(0, 1)})
    down = ({"section": at(3, 0)}, {"section": at(0, 3)})

    sends, indices, local = [], iter(range(send_sem.shape[0])), iter(range(load_sem.shape[0]))

    def go(src, dst, to):
        index = next(indices)
        c = pltpu.make_async_remote_copy(
            src_ref=src, dst_ref=dst, send_sem=send_sem.at[index], recv_sem=recv_sem.at[index],
            device_id=to, device_id_type=MESH,
        )
        c.start()
        sends.append(c)
        return c

    def move(src, dst):
        c = pltpu.make_async_copy(src, dst, load_sem.at[next(local)])
        c.start()
        return c

    own_grads = move(grad_ref, grads.at[0, z])
    loads = [
        move(wq_ref, weights.at[0, 0]),
        move(wk_ref, weights.at[0, 1]),
        move(wv_ref, weights.at[0, 2]),
        move(wo_ref, out_weights.at[0]),
    ]
    load_pending = move(pending_ref, pending)

    barrier = pltpu.get_barrier_semaphore()
    friends = (right, left, across, twin) + up + down
    for friend in friends:
        pl.semaphore_signal(barrier, inc=1, device_id=friend, device_id_type=MESH)
    pl.semaphore_wait(barrier, len(friends))

    w_twin = []
    lo, hi = pl.ds(0, half), pl.ds(half, half)
    quarter = [pl.ds(i * SLAB, SLAB) for i in range(rows // SLAB)]
    sent = {}

    def normalize():
        def one(i, carry):
            here = pl.ds(pl.multiple_of(i * 16, 16), 16)
            values = saved_ref[here, :].astype(f32)
            factor = lax.rsqrt(jnp.mean(values * values, axis=-1, keepdims=True) + eps)
            normed[0, z, here, :] = (values * factor * gain_ref[...]).astype(bf16)
            return carry

        lax.fori_loop(0, rows // 16, one, 0)
        for j, w in enumerate((wq_ref, wk_ref, wv_ref)):
            w_twin.append(go(w, weights.at[1, j], twin))
        w_twin.append(go(wo_ref, out_weights.at[1], twin))

    def place_of(r):
        return pl.ds(pl.multiple_of(lax.rem(x + 4 - r, 4) * pair, pair), pair)

    results = []

    def hand_over(r, first, count):
        js, here = pl.ds(first, count), place_of(r)
        results.append(go(theirs.at[js, here], heads.at[core, js, here], twin))

    def project(r, which):
        if r == 0:
            for c in (w_twin if which else loads)[:3]:
                c.wait_recv() if which else c.wait()
        here = place_of(r)

        def one(j, carry):
            product = dot(normed[r].reshape(pair, depth), weights[which, j], 1, 0).astype(bf16)
            if which == 0:
                heads[core, j, here, :] = product
            else:
                theirs[j, here, :] = product
            return carry

        lax.fori_loop(0, 3, one, 0)
        if which == 1:
            hand_over(r, 0, 3)

    def project_grads(r):
        if r == 0:
            own_grads.wait()
            loads[3].wait()
            w_twin[3].wait_recv()
        here = place_of(r)
        for which in (1, 0):
            product = dot(grads[r].reshape(pair, depth), out_weights[which], 1, 1).astype(bf16)
            if which == 0:
                heads[core, 3, here, :] = product
            else:
                theirs[3, here, :] = product
                hand_over(r, 3, 1)

    mine, crossed = normed.at[0, z], normed.at[0, other]
    moves = {
        "gA": ((), grad_ref, grads.at[0, z], across),
        "nA": ((), mine, mine, across),
        "gxR": (("gRlo",), grads.at[1, z, lo], grads.at[2, z, lo], right),
        "gxL": (("gLhi",), grads.at[3, z, hi], grads.at[2, z, hi], left),
        "nxR": (("nRlo",), normed.at[1, z, lo], normed.at[2, z, lo], right),
        "nxL": (("nLhi",), normed.at[3, z, hi], normed.at[2, z, hi], left),
        "oxR": (("oRlo",), normed.at[1, other, lo], normed.at[2, other, lo], right),
        "oxL": (("oLhi",), normed.at[3, other, hi], normed.at[2, other, hi], left),
        "g1A": (("gRlo", "gRhi"), grads.at[1, z], grads.at[1, z], across),
        "g3A": (("gLlo", "gLhi"), grads.at[3, z], grads.at[3, z], across),
        "g2Alo": (("gxR",), grads.at[2, z, quarter[1]], grads.at[2, z, quarter[1]], across),
        "g2Ahi": (("gxL",), grads.at[2, z, quarter[2]], grads.at[2, z, quarter[2]], across),
        "zxR": (("g1A",), grads.at[1, other, quarter[0]], grads.at[2, other, quarter[0]], right),
        "zxL": (("g3A",), grads.at[3, other, quarter[3]], grads.at[2, other, quarter[3]], left),
    }
    for end, part_rows in (("lo", lo), ("hi", hi)):
        for way, r, to in (("R", 1, right), ("L", 3, left)):
            moves["g" + way + end] = ((), grad_ref.at[part_rows], grads.at[r, z, part_rows], to)
            moves["n" + way + end] = ((), mine.at[part_rows], normed.at[r, z, part_rows], to)
            moves["o" + way + end] = (("nA",), crossed.at[part_rows], normed.at[r, other, part_rows], to)
    needs = {
        "P0": ("nA",), "P1": ("nRlo", "nRhi", "oRlo", "oRhi"), "P3": ("nLlo", "nLhi", "oLlo", "oLhi"),
        "P2": ("nxR", "nxL", "oxR", "oxL"), "G0": ("gA",), "G1": ("gRlo", "gRhi", "g1A"),
        "G3": ("gLlo", "gLhi", "g3A"), "G2": ("gxR", "gxL", "g2Alo", "g2Ahi", "zxR", "zxL"),
    }
    landed = set()

    def need(names):
        for name in names:
            if name not in landed:
                landed.add(name)
                sent[name].wait_recv()

    for name in GATHER:
        if name == "nrm":
            normalize()
        elif name in moves:
            waits, src, dst, to = moves[name]
            need(waits)
            sent[name] = go(src, dst, to)
        else:
            need(needs[name[:2]])
            if name[0] == "P":
                project(int(name[1]), 1 if name.endswith("t") else 0)
            else:
                project_grads(int(name[1]))
    for c in results:
        c.wait_recv()

    tokens = q_ref.shape[0]
    block = 256
    chips = tokens // pair
    scale = 1.0 / math.sqrt(HEAD)
    places = [(chip, c) for chip in range(chips) for c in (0, 1)]
    for j, ref in enumerate((q_ref, k_ref, v_ref, g_ref)):
        for chip, c in places:
            ref[pl.ds((2 * chip + c) * rows, rows), :] = heads[c, j, pl.ds(chip * rows, rows), :]
    below = lax.broadcasted_iota(jnp.int32, (block, block), 0) <= lax.broadcasted_iota(
        jnp.int32, (block, block), 1
    )

    def put(j, chip, c, cols, value):
        for s in range(rows // SLAB):
            there = pl.ds((s * chips + chip) * SLAB, SLAB)
            back[c, j, there, cols] = value[s * SLAB : (s + 1) * SLAB].astype(bf16)

    swaps = []
    for head in range(width // HEAD):
        cols = pl.ds(head * HEAD, HEAD)
        keys_t = k_ref[:, cols].T
        values_t = v_ref[:, cols].T
        for step in reversed(range(tokens // block)):
            n = (step + 1) * block
            mine = pl.ds(step * block, block)
            query, grad = q_ref[mine, cols], g_ref[mine, cols]
            scores = dot(k_ref[pl.ds(0, n), cols], query, 1, 1) * (scale * math.log2(math.e))
            last = jnp.where(below, scores[n - block :], -1e30)
            scores = last if step == 0 else jnp.concatenate((scores[: n - block], last), axis=0)
            peak = jnp.max(scores, axis=0, keepdims=True)
            exps = jnp.exp2(scores - peak)
            exps = exps * (1.0 / jnp.sum(exps, axis=0, keepdims=True))
            probs = exps.astype(bf16)
            output_t = dot(values_t[:, :n], probs, 1, 0)
            delta = jnp.sum(grad.astype(f32).T * output_t, axis=0, keepdims=True)
            grad_probs = dot(v_ref[pl.ds(0, n), cols], grad, 1, 1)
            grad_scores = (exps * ((grad_probs - delta) * scale)).astype(bf16)
            grad_query = dot(keys_t[:, :n], grad_scores, 1, 0).T
            for chip, c in places:
                offset = (2 * chip + c) * rows - step * block
                if 0 <= offset < block:
                    put(0, chip, c, cols, grad_query[offset : offset + rows])
            more_k = dot(grad_scores, query, 1, 0)
            more_v = dot(probs, grad, 1, 0)
            if step == tokens // block - 1:
                dk_acc[...] = more_k
                dv_acc[...] = more_v
            else:
                dk_acc[pl.ds(0, n)] += more_k
                dv_acc[pl.ds(0, n)] += more_v
        for j, acc in ((1, dk_acc), (2, dv_acc)):
            for chip, c in places:
                put(j, chip, c, cols, acc[pl.ds((2 * chip + c) * rows, rows), :])
        everything = pl.ds(0, tokens // 2)
        swaps.append(go(back.at[1 - core, :, everything, cols], back_twin.at[:, everything, cols], twin))

    slabs = rows // SLAB
    chunk = 512
    together = chips * SLAB

    def coefficient(j, s):
        return jnp.where(s > j, alpha_ref[s, j], 0.0)

    coeffs = {}
    for r in range(4):
        for t in range(4):
            coeffs[0, r, t] = coefficient(at(0, r), at(4 - t, 0))
            coeffs[1, r, t] = coefficient(at(r, 0), at(0, 4 - t))

    def spot(r):
        return lax.rem(x + r, 4)

    def plus(target, source):
        target[...] = (target[...].astype(f32) + source[...].astype(f32)).astype(bf16)

    live = {}

    def product(s):
        here = pl.ds(s * together, 2 * together)

        def step(n, carry):
            cols = pl.ds(pl.multiple_of(n * chunk, chunk), chunk)
            total = dot(back[core, 0, here, :], weights[0, 0, cols, :], 1, 1)
            for j in (1, 2):
                total += dot(back[core, j, here, :], weights[0, j, cols, :], 1, 1)
            for j in (0, 1, 2):
                total += dot(back_twin[j, here, :], weights[1, j, cols, :], 1, 1)
            part[s : s + 2, :, :, :, cols] = total.astype(bf16).reshape(2, chips // 2, 2, SLAB, chunk)
            return carry

        lax.fori_loop(0, depth // chunk, step, 0)

    def first(s):
        live["x1r", s] = go(part.at[s, spot(2), 0], xb1.at[s, 0], right)
        live["x1l", s] = go(part.at[s, spot(2), 1], xb1.at[s, 1], left)
        live["x2", s] = [
            go(part.at[s, spot(1), 1], xb2.at[s, 0, 1], right),
            go(part.at[s, spot(3), 0], xb2.at[s, 1, 0], left),
        ]

    def second(s):
        live["x1r", s].wait_recv()
        plus(part.at[s, spot(1), 0], xb1.at[s, 0])
        live["x2", s].append(go(part.at[s, spot(1), 0], xb2.at[s, 0, 0], right))
        live["x1l", s].wait_recv()
        plus(part.at[s, spot(3), 1], xb1.at[s, 1])
        live["x2", s].append(go(part.at[s, spot(3), 1], xb2.at[s, 1, 1], left))

    def cross(s):
        for c in live["x2", s]:
            c.wait_recv()
        total = part[s, x, other].astype(f32) + xb2[s, 0, other].astype(f32) + xb2[s, 1, other].astype(f32)
        part[s, x, other] = total.astype(bf16)
        live["z", s] = go(part.at[s, x, other], zb.at[s], across)

    def norm_back(s):
        live["z", s].wait_recv()
        here = pl.ds(s * SLAB, SLAB)
        saved = saved_ref[here, :].astype(f32)
        total = part[s, x, z].astype(f32) + xb2[s, 0, z].astype(f32)
        total = total + xb2[s, 1, z].astype(f32) + zb[s].astype(f32)
        factor = lax.rsqrt(jnp.mean(saved * saved, axis=-1, keepdims=True) + eps)
        scaled = total * gain_ref[...]
        inner = jnp.mean(scaled * saved, axis=-1, keepdims=True)
        change = factor * (scaled - saved * (factor * factor * inner))
        value = (grads[0, z, here, :].astype(f32) + change).astype(bf16)
        in_grads_ref[here, :] = value
        for w in (0, 1):
            source = in_grads_ref.at[here, pl.ds(w * wide, wide)]
            live["g", s, w] = (
                go(source, gather.at[s, w, 0], up[w]),
                go(source, gather.at[s, w, 2], down[w]),
            )

    lower, upper = pl.ds(0, narrow), pl.ds(narrow, narrow)
    all_rows = pl.ds(0, SLAB)

    def relay(s, w):
        one, three = live["g", s, w]
        one.wait_recv()
        a = go(gather.at[s, w, 0, all_rows, lower], gather.at[s, w, 1, all_rows, lower], up[w])
        three.wait_recv()
        b = go(gather.at[s, w, 2, all_rows, upper], gather.at[s, w, 1, all_rows, upper], down[w])
        live["r", s, w] = (a, b)

    def sums(s, w):
        for c in live["r", s, w]:
            c.wait_recv()

        def body(i, carry):
            cols = pl.ds(pl.multiple_of(i * 256, 256), 256)
            own = pl.ds(pl.multiple_of(w * wide + i * 256, 256), 256)
            blocks = [in_grads_ref[pl.ds(s * SLAB, SLAB), own].astype(f32)]
            blocks += [gather[s, w, t, :, cols].astype(f32) for t in range(3)]
            for r in range(4):
                total = blocks[0] * coeffs[w, r, 0]
                for t in (1, 2, 3):
                    total = total + blocks[t] * coeffs[w, r, t]
                if r == 0:
                    kept[s, w, :, cols] = total
                else:
                    stage[s, w, r - 1, :, cols] = total.astype(bf16)
            return carry

        lax.fori_loop(0, wide // 256, body, 0)
        u, d = up[1 - w], down[1 - w]
        live["p", s, w] = (
            go(stage.at[s, w, 1, all_rows, lower], arrived.at[s, w, 2, all_rows, lower], u),
            go(stage.at[s, w, 1, all_rows, upper], arrived.at[s, w, 2, all_rows, upper], d),
        )
        live["q", s, w] = [
            go(stage.at[s, w, 0, all_rows, upper], arrived.at[s, w, 0, all_rows, upper], u),
            go(stage.at[s, w, 2, all_rows, lower], arrived.at[s, w, 1, all_rows, lower], d),
        ]

    def late(s, w):
        a, b = live["p", s, w]
        u, d = up[1 - w], down[1 - w]
        a.wait_recv()
        plus(stage.at[s, w, 0, all_rows, lower], arrived.at[s, w, 2, all_rows, lower])
        live["q", s, w].append(
            go(stage.at[s, w, 0, all_rows, lower], arrived.at[s, w, 0, all_rows, lower], u)
        )
        b.wait_recv()
        plus(stage.at[s, w, 2, all_rows, upper], arrived.at[s, w, 2, all_rows, upper])
        live["q", s, w].append(
            go(stage.at[s, w, 2, all_rows, upper], arrived.at[s, w, 1, all_rows, upper], d)
        )

    def finish(s):
        here = pl.ds(s * SLAB, SLAB)
        for w in (1, 0):
            for c in live["q", s, w]:
                c.wait_recv()
            cols = pl.ds(w * wide, wide)
            total = pending[here, cols].astype(f32) + kept[s, w]
            total = total + arrived[s, w, 0].astype(f32) + arrived[s, w, 1].astype(f32)
            updated_ref[here, cols] = total.astype(bf16)

    stages = {
        "product": product, "first": first, "second": second, "across": cross, "norm": norm_back,
        "relay_y": lambda s: relay(s, 0), "relay_z": lambda s: relay(s, 1),
        "sums_y": lambda s: sums(s, 0), "sums_z": lambda s: sums(s, 1),
        "late_y": lambda s: late(s, 0), "late_z": lambda s: late(s, 1), "finish": finish,
    }
    for c in swaps:
        c.wait_recv()
    load_pending.wait()
    for name in SUMS:
        stages[name[:-1]](int(name[-1]))
    for c in sends:
        c.wait_send()


def on_device(saved_in, out_grad, pending, gain, alpha, w_query, w_key, w_value, w_out):
    _, rows, depth = saved_in.shape
    width = w_query.shape[2]
    tokens = 16 * rows
    slabs = rows // SLAB
    wide = depth // 2
    vmem = pl.BlockSpec(memory_space=pltpu.VMEM)
    smem = pl.BlockSpec(memory_space=pltpu.SMEM)
    hbm = pl.BlockSpec(memory_space=pl.ANY)
    rows_out = jax.ShapeDtypeStruct((rows, depth), bf16)

    def buffer(*shape):
        return pltpu.VMEM(shape, bf16)

    grad_input, updated = pl.pallas_call(
        kernel,
        out_shape=(rows_out, rows_out),
        in_specs=[smem, vmem, vmem, hbm, hbm, hbm, hbm, hbm, hbm],
        out_specs=(vmem, vmem),
        scratch_shapes=[
            buffer(4, 2, rows, depth),
            buffer(4, 2, rows, depth),
            buffer(2, 3, depth, width),
            buffer(2, width, depth),
            buffer(4, tokens // 2, width),
            buffer(2, 4, tokens // 2, width),
            buffer(tokens, width),
            buffer(tokens, width),
            buffer(tokens, width),
            buffer(tokens, width),
            pltpu.VMEM((tokens, HEAD), f32),
            pltpu.VMEM((tokens, HEAD), f32),
            buffer(2, 3, tokens // 2, width),
            buffer(3, tokens // 2, width),
            buffer(slabs, 4, 2, SLAB, depth),
            buffer(slabs, 2, SLAB, depth),
            buffer(slabs, 2, 2, SLAB, depth),
            buffer(slabs, SLAB, depth),
            buffer(rows, depth),
            buffer(slabs, 2, 3, SLAB, wide),
            buffer(slabs, 2, 3, SLAB, wide),
            buffer(slabs, 2, 3, SLAB, wide),
            pltpu.VMEM((slabs, 2, SLAB, wide), f32),
            pltpu.SemaphoreType.DMA((40 + 27 * slabs,)),
            pltpu.SemaphoreType.DMA((40 + 27 * slabs,)),
            pltpu.SemaphoreType.DMA((6,)),
        ],
        compiler_params=pltpu.CompilerParams(
            collective_id=1, has_side_effects=True, vmem_limit_bytes=52 * 2**20
        ),
        cost_estimate=pl.CostEstimate(flops=14 * 10**9, bytes_accessed=10**7, transcendentals=10**6),
    )(alpha, saved_in[0], gain, out_grad[0], pending[0], w_query[0], w_key[0], w_value[0], w_out[0])
    return (grad_input[None], updated[None])


def solution(mesh):
    return jax.shard_map(
        on_device,
        mesh=mesh,
        in_specs=(
            P("section", "tp", None),
            P("section", "tp", None),
            P("section", "tp", None),
            P("section", None),
            P(),
            P("section", None, "tp"),
            P("section", None, "tp"),
            P("section", None, "tp"),
            P("section", "tp", None),
        ),
        out_specs=(P("section", "tp", None), P("section", "tp", None)),
        check_vma=False,
    )
```

```python
import math

import jax
import jax.numpy as jnp
from jax import lax
from jax.experimental import pallas as pl
from jax.experimental.pallas import tpu as pltpu
from jax.sharding import PartitionSpec as P

HEAD = 128
SLAB = 16
MESH = pl.DeviceIdType.MESH

eps = 1e-05

f32, bf16 = jnp.float32, jnp.bfloat16

GATHER = (
    "gLlo", "gRlo", "gA", "nrm", "nRhi", "gLhi", "nLlo", "gxR", "nLhi", "nA", "nRlo", "gxL", "gRhi",
    "g3A", "oRlo", "oLhi", "P0t", "P0", "oRhi", "oLlo", "g1A", "G0", "G3", "oxL", "nxR", "oxR",
    "P1t", "g2Ahi", "P3t", "nxL", "P3", "P1", "g2Alo", "G1", "zxR", "zxL", "P2t", "P2", "G2",
)
SUMS = (
    "product0", "first1", "first0", "product2", "second1", "across1", "second0", "across0", "norm1",
    "first2", "norm0", "relay_z1", "relay_y1", "first3", "relay_y0", "sums_y1", "second2",
    "relay_z0", "sums_z1", "sums_y0", "second3", "across2", "sums_z0", "late_z1", "across3",
    "norm2", "late_z0", "norm3", "relay_z2", "relay_y3", "relay_y2", "late_y1", "relay_z3",
    "sums_y3", "sums_z2", "sums_y2", "sums_z3", "finish1", "late_y3", "late_y0", "late_z2",
    "late_y2", "late_z3", "finish0", "finish3", "finish2",
)
ACROSS_FIRST = (0,)


def dot(a, b, ca, cb):
    return lax.dot_general(a, b, (((ca,), (cb,)), ((), ())), preferred_element_type=f32)


def neighbours():
    place = lax.axis_index("tp")
    x, z, core = place // 4, lax.rem(place // 2, 2), lax.rem(place, 2)
    right = lax.rem(x + 1, 4) * 4 + z * 2 + core
    left = lax.rem(x + 3, 4) * 4 + z * 2 + core
    across = x * 4 + (1 - z) * 2 + core
    twin = x * 4 + z * 2 + (1 - core)
    return x, z, core, {"tp": right}, {"tp": left}, {"tp": across}, {"tp": twin}


def kernel(alpha_in, saved_in, gain_in, grad_ref, pending_ref, wq_ref, wk_ref, wv_ref, wo_ref,
           in_grads_ref, updated_ref,
           alpha_ref, saved_ref, gain_ref, normed, grads, weights, out_weights, theirs, heads,
           q_ref, k_ref, v_ref, g_ref, dk_acc, dv_acc,
           back, back_twin, part, xb1, xb2, za, zb,
           pending, gather, stage, arrived, kept,
           send_sem, recv_sem, load_sem):
    x, z, core, right, left, across, twin = neighbours()
    section = lax.axis_index("section")
    y, zh = section // 4, lax.rem(section, 4)
    rows, depth = saved_ref.shape
    width = wq_ref.shape[1]
    pair, half = 2 * rows, rows // 2
    wide = depth // 2
    narrow = wide // 2
    other = 1 - z

    def at(dy, dz):
        return lax.rem(y + dy + 4, 4) * 4 + lax.rem(zh + dz + 4, 4)

    up = ({"section": at(1, 0)}, {"section": at(0, 1)})
    down = ({"section": at(3, 0)}, {"section": at(0, 3)})

    sends, indices, local = [], iter(range(send_sem.shape[0])), iter(range(load_sem.shape[0]))

    def go(src, dst, to):
        index = next(indices)
        c = pltpu.make_async_remote_copy(
            src_ref=src, dst_ref=dst, send_sem=send_sem.at[index], recv_sem=recv_sem.at[index],
            device_id=to, device_id_type=MESH,
        )
        c.start()
        sends.append(c)
        return c

    def move(src, dst):
        c = pltpu.make_async_copy(src, dst, load_sem.at[next(local)])
        c.start()
        return c

    load_rows = [move(saved_in, saved_ref), move(gain_in, gain_ref)]
    own_grads = move(grad_ref, grads.at[0, z])
    loads = [
        move(wq_ref, weights.at[0, 0]),
        move(wk_ref, weights.at[0, 1]),
        move(wv_ref, weights.at[0, 2]),
        move(wo_ref, out_weights.at[0]),
    ]
    load_late = [move(pending_ref, pending), move(alpha_in, alpha_ref)]

    barrier = pltpu.get_barrier_semaphore()
    friends = (right, left, across, twin) + up + down
    for friend in friends:
        pl.semaphore_signal(barrier, inc=1, device_id=friend, device_id_type=MESH)
    pl.semaphore_wait(barrier, len(friends))

    w_twin = []
    lo, hi = pl.ds(0, half), pl.ds(half, half)
    quarter = [pl.ds(i * SLAB, SLAB) for i in range(rows // SLAB)]
    sent = {}

    def normalize():
        for c in load_rows:
            c.wait()

        def one(i, carry):
            here = pl.ds(pl.multiple_of(i * 16, 16), 16)
            values = saved_ref[here, :].astype(f32)
            factor = lax.rsqrt(jnp.mean(values * values, axis=-1, keepdims=True) + eps)
            normed[0, z, here, :] = (values * factor * gain_ref[...]).astype(bf16)
            return carry

        lax.fori_loop(0, rows // 16, one, 0)
        for j, w in enumerate((wq_ref, wk_ref, wv_ref)):
            w_twin.append(go(w, weights.at[1, j], twin))
        w_twin.append(go(wo_ref, out_weights.at[1], twin))

    def place_of(r):
        return pl.ds(pl.multiple_of(lax.rem(x + 4 - r, 4) * pair, pair), pair)

    results = []

    def hand_over(r, first, count):
        js, here = pl.ds(first, count), place_of(r)
        results.append(go(theirs.at[js, here], heads.at[core, js, here], twin))

    def project(r, which):
        if r == 0:
            for c in (w_twin if which else loads)[:3]:
                c.wait_recv() if which else c.wait()
        here = place_of(r)

        def one(j, carry):
            product = dot(normed[r].reshape(pair, depth), weights[which, j], 1, 0).astype(bf16)
            if which == 0:
                heads[core, j, here, :] = product
            else:
                theirs[j, here, :] = product
            return carry

        lax.fori_loop(0, 3, one, 0)
        if which == 1:
            hand_over(r, 0, 3)

    def project_grads(r):
        if r == 0:
            own_grads.wait()
            loads[3].wait()
            w_twin[3].wait_recv()
        here = place_of(r)
        for which in (1, 0):
            product = dot(grads[r].reshape(pair, depth), out_weights[which], 1, 1).astype(bf16)
            if which == 0:
                heads[core, 3, here, :] = product
            else:
                theirs[3, here, :] = product
                hand_over(r, 3, 1)

    mine, crossed = normed.at[0, z], normed.at[0, other]
    moves = {
        "gA": ((), grad_ref, grads.at[0, z], across),
        "nA": ((), mine, mine, across),
        "gxR": (("gRlo",), grads.at[1, z, lo], grads.at[2, z, lo], right),
        "gxL": (("gLhi",), grads.at[3, z, hi], grads.at[2, z, hi], left),
        "nxR": (("nRlo",), normed.at[1, z, lo], normed.at[2, z, lo], right),
        "nxL": (("nLhi",), normed.at[3, z, hi], normed.at[2, z, hi], left),
        "oxR": (("oRlo",), normed.at[1, other, lo], normed.at[2, other, lo], right),
        "oxL": (("oLhi",), normed.at[3, other, hi], normed.at[2, other, hi], left),
        "g1A": (("gRlo", "gRhi"), grads.at[1, z], grads.at[1, z], across),
        "g3A": (("gLlo", "gLhi"), grads.at[3, z], grads.at[3, z], across),
        "g2Alo": (("gxR",), grads.at[2, z, quarter[1]], grads.at[2, z, quarter[1]], across),
        "g2Ahi": (("gxL",), grads.at[2, z, quarter[2]], grads.at[2, z, quarter[2]], across),
        "zxR": (("g1A",), grads.at[1, other, quarter[0]], grads.at[2, other, quarter[0]], right),
        "zxL": (("g3A",), grads.at[3, other, quarter[3]], grads.at[2, other, quarter[3]], left),
    }
    for end, part_rows in (("lo", lo), ("hi", hi)):
        for way, r, to in (("R", 1, right), ("L", 3, left)):
            moves["g" + way + end] = ((), grad_ref.at[part_rows], grads.at[r, z, part_rows], to)
            moves["n" + way + end] = ((), mine.at[part_rows], normed.at[r, z, part_rows], to)
            moves["o" + way + end] = (("nA",), crossed.at[part_rows], normed.at[r, other, part_rows], to)
    needs = {
        "P0": ("nA",), "P1": ("nRlo", "nRhi", "oRlo", "oRhi"), "P3": ("nLlo", "nLhi", "oLlo", "oLhi"),
        "P2": ("nxR", "nxL", "oxR", "oxL"), "G0": ("gA",), "G1": ("gRlo", "gRhi", "g1A"),
        "G3": ("gLlo", "gLhi", "g3A"), "G2": ("gxR", "gxL", "g2Alo", "g2Ahi", "zxR", "zxL"),
    }
    landed = set()

    def need(names):
        for name in names:
            if name not in landed:
                landed.add(name)
                sent[name].wait_recv()

    for name in GATHER:
        if name == "nrm":
            normalize()
        elif name in moves:
            waits, src, dst, to = moves[name]
            need(waits)
            sent[name] = go(src, dst, to)
        else:
            need(needs[name[:2]])
            if name[0] == "P":
                project(int(name[1]), 1 if name.endswith("t") else 0)
            else:
                project_grads(int(name[1]))
    for c in results:
        c.wait_recv()

    tokens = q_ref.shape[0]
    block = 512
    chips = tokens // pair
    scale = 1.0 / math.sqrt(HEAD)
    places = [(chip, c) for chip in range(chips) for c in (0, 1)]
    for j, ref in enumerate((q_ref, k_ref, v_ref, g_ref)):
        for chip, c in places:
            ref[pl.ds((2 * chip + c) * rows, rows), :] = heads[c, j, pl.ds(chip * rows, rows), :]
    below = lax.broadcasted_iota(jnp.int32, (block, block), 0) <= lax.broadcasted_iota(
        jnp.int32, (block, block), 1
    )

    def put(j, chip, c, cols, value):
        for s in range(rows // SLAB):
            there = pl.ds((s * chips + chip) * SLAB, SLAB)
            back[c, j, there, cols] = value[s * SLAB : (s + 1) * SLAB].astype(bf16)

    swaps = []
    for head in range(width // HEAD):
        cols = pl.ds(head * HEAD, HEAD)
        keys_t = k_ref[:, cols].T
        values_t = v_ref[:, cols].T
        for step in reversed(range(tokens // block)):
            n = (step + 1) * block
            mine = pl.ds(step * block, block)
            query, grad = q_ref[mine, cols], g_ref[mine, cols]
            scores = dot(k_ref[pl.ds(0, n), cols], query, 1, 1) * (scale * math.log2(math.e))
            last = jnp.where(below, scores[n - block :], -1e30)
            scores = last if step == 0 else jnp.concatenate((scores[: n - block], last), axis=0)
            peak = jnp.max(scores, axis=0, keepdims=True)
            exps = jnp.exp2(scores - peak)
            exps = exps * (1.0 / jnp.sum(exps, axis=0, keepdims=True))
            probs = exps.astype(bf16)
            output_t = dot(values_t[:, :n], probs, 1, 0)
            delta = jnp.sum(grad.astype(f32).T * output_t, axis=0, keepdims=True)
            grad_probs = dot(v_ref[pl.ds(0, n), cols], grad, 1, 1)
            grad_scores = (exps * ((grad_probs - delta) * scale)).astype(bf16)
            grad_query = dot(keys_t[:, :n], grad_scores, 1, 0).T
            for chip, c in places:
                offset = (2 * chip + c) * rows - step * block
                if 0 <= offset < block:
                    put(0, chip, c, cols, grad_query[offset : offset + rows])
            more_k = dot(grad_scores, query, 1, 0)
            more_v = dot(probs, grad, 1, 0)
            if step == tokens // block - 1:
                dk_acc[...] = more_k
                dv_acc[...] = more_v
            else:
                dk_acc[pl.ds(0, n)] += more_k
                dv_acc[pl.ds(0, n)] += more_v
        for j, acc in ((1, dk_acc), (2, dv_acc)):
            for chip, c in places:
                put(j, chip, c, cols, acc[pl.ds((2 * chip + c) * rows, rows), :])
        everything = pl.ds(0, tokens // 2)
        swaps.append(go(back.at[1 - core, :, everything, cols], back_twin.at[:, everything, cols], twin))

    slabs = rows // SLAB
    all_rows = pl.ds(0, SLAB)
    chunk = 512
    together = chips * SLAB

    def coefficient(j, s):
        return jnp.where(s > j, alpha_ref[s, j], 0.0)

    for c in load_late:
        c.wait()
    coeffs = {}
    for r in range(4):
        for t in range(4):
            coeffs[0, r, t] = coefficient(at(0, r), at(4 - t, 0))
            coeffs[1, r, t] = coefficient(at(r, 0), at(0, 4 - t))

    def spot(r):
        return lax.rem(x + r, 4)

    def plus(target, source):
        target[...] = (target[...].astype(f32) + source[...].astype(f32)).astype(bf16)

    live = {}

    def product(s):
        here = pl.ds(s * together, 2 * together)

        def step(n, carry):
            cols = pl.ds(pl.multiple_of(n * chunk, chunk), chunk)
            total = dot(back[core, 0, here, :], weights[0, 0, cols, :], 1, 1)
            for j in (1, 2):
                total += dot(back[core, j, here, :], weights[0, j, cols, :], 1, 1)
            for j in (0, 1, 2):
                total += dot(back_twin[j, here, :], weights[1, j, cols, :], 1, 1)
            part[s : s + 2, :, :, :, cols] = total.astype(bf16).reshape(2, chips // 2, 2, SLAB, chunk)
            return carry

        lax.fori_loop(0, depth // chunk, step, 0)

    early, latter = pl.ds(0, wide), pl.ds(wide, wide)

    def first(s):
        if s in ACROSS_FIRST:
            for r in (2, 1, 3, 0):
                live["za", s, r] = go(part.at[s, spot(r), other], za.at[r], across)
            return
        live["x1r", s] = go(part.at[s, spot(2), 0], xb1.at[s, 0], right)
        live["x1l", s] = go(part.at[s, spot(2), 1], xb1.at[s, 1], left)
        live["x2", s] = [
            go(part.at[s, spot(1), 1], xb2.at[s, 0, 1], right),
            go(part.at[s, spot(3), 0], xb2.at[s, 1, 0], left),
        ]

    def second(s):
        if s in ACROSS_FIRST:
            two, one, three = (part.at[s, spot(r), z] for r in (2, 1, 3))
            live["za", s, 2].wait_recv()
            plus(two, za.at[2])
            live["x1r", s] = go(two.at[all_rows, early], xb1.at[s, 0, all_rows, early], right)
            live["x1l", s] = go(two.at[all_rows, latter], xb1.at[s, 0, all_rows, latter], left)
            live["za", s, 1].wait_recv()
            plus(one, za.at[1])
            live["x2", s] = [go(one.at[all_rows, latter], xb2.at[s, 0, 0, all_rows, latter], right)]
            live["za", s, 3].wait_recv()
            plus(three, za.at[3])
            live["x2", s].append(go(three.at[all_rows, early], xb2.at[s, 1, 0, all_rows, early], left))
            return
        live["x1r", s].wait_recv()
        plus(part.at[s, spot(1), 0], xb1.at[s, 0])
        live["x2", s].append(go(part.at[s, spot(1), 0], xb2.at[s, 0, 0], right))
        live["x1l", s].wait_recv()
        plus(part.at[s, spot(3), 1], xb1.at[s, 1])
        live["x2", s].append(go(part.at[s, spot(3), 1], xb2.at[s, 1, 1], left))

    def cross(s):
        if s in ACROSS_FIRST:
            one, three = (part.at[s, spot(r), z] for r in (1, 3))
            live["x1r", s].wait_recv()
            plus(one.at[all_rows, early], xb1.at[s, 0, all_rows, early])
            live["x2", s].append(go(one.at[all_rows, early], xb2.at[s, 0, 0, all_rows, early], right))
            live["x1l", s].wait_recv()
            plus(three.at[all_rows, latter], xb1.at[s, 0, all_rows, latter])
            live["x2", s].append(go(three.at[all_rows, latter], xb2.at[s, 1, 0, all_rows, latter], left))
            return
        for c in live["x2", s]:
            c.wait_recv()
        total = part[s, x, other].astype(f32) + xb2[s, 0, other].astype(f32) + xb2[s, 1, other].astype(f32)
        part[s, x, other] = total.astype(bf16)
        live["z", s] = go(part.at[s, x, other], zb.at[s], across)

    def norm_back(s):
        here = pl.ds(s * SLAB, SLAB)
        if s in ACROSS_FIRST:
            for c in live["x2", s] + [live["za", s, 0]]:
                c.wait_recv()
        else:
            live["z", s].wait_recv()
        saved = saved_ref[here, :].astype(f32)
        last, k = (za[0], 0) if s in ACROSS_FIRST else (zb[s], z)
        total = part[s, x, z].astype(f32) + xb2[s, 0, k].astype(f32)
        total = total + xb2[s, 1, k].astype(f32) + last.astype(f32)
        factor = lax.rsqrt(jnp.mean(saved * saved, axis=-1, keepdims=True) + eps)
        scaled = total * gain_ref[...]
        inner = jnp.mean(scaled * saved, axis=-1, keepdims=True)
        change = factor * (scaled - saved * (factor * factor * inner))
        value = (grads[0, z, here, :].astype(f32) + change).astype(bf16)
        in_grads_ref[here, :] = value
        for w in (0, 1):
            source = in_grads_ref.at[here, pl.ds(w * wide, wide)]
            live["g", s, w] = (
                go(source, gather.at[s, w, 0], up[w]),
                go(source, gather.at[s, w, 2], down[w]),
            )

    lower, upper = pl.ds(0, narrow), pl.ds(narrow, narrow)

    def relay(s, w):
        one, three = live["g", s, w]
        one.wait_recv()
        a = go(gather.at[s, w, 0, all_rows, lower], gather.at[s, w, 1, all_rows, lower], up[w])
        three.wait_recv()
        b = go(gather.at[s, w, 2, all_rows, upper], gather.at[s, w, 1, all_rows, upper], down[w])
        live["r", s, w] = (a, b)

    def sums(s, w):
        for c in live["r", s, w]:
            c.wait_recv()

        def body(i, carry):
            cols = pl.ds(pl.multiple_of(i * 256, 256), 256)
            own = pl.ds(pl.multiple_of(w * wide + i * 256, 256), 256)
            blocks = [in_grads_ref[pl.ds(s * SLAB, SLAB), own].astype(f32)]
            blocks += [gather[s, w, t, :, cols].astype(f32) for t in range(3)]
            for r in range(4):
                total = blocks[0] * coeffs[w, r, 0]
                for t in (1, 2, 3):
                    total = total + blocks[t] * coeffs[w, r, t]
                if r == 0:
                    kept[s, w, :, cols] = total
                else:
                    stage[s, w, r - 1, :, cols] = total.astype(bf16)
            return carry

        lax.fori_loop(0, wide // 256, body, 0)
        u, d = up[1 - w], down[1 - w]
        live["p", s, w] = (
            go(stage.at[s, w, 1, all_rows, lower], arrived.at[s, w, 2, all_rows, lower], u),
            go(stage.at[s, w, 1, all_rows, upper], arrived.at[s, w, 2, all_rows, upper], d),
        )
        live["q", s, w] = [
            go(stage.at[s, w, 0, all_rows, upper], arrived.at[s, w, 0, all_rows, upper], u),
            go(stage.at[s, w, 2, all_rows, lower], arrived.at[s, w, 1, all_rows, lower], d),
        ]

    def late(s, w):
        a, b = live["p", s, w]
        u, d = up[1 - w], down[1 - w]
        a.wait_recv()
        plus(stage.at[s, w, 0, all_rows, lower], arrived.at[s, w, 2, all_rows, lower])
        live["q", s, w].append(
            go(stage.at[s, w, 0, all_rows, lower], arrived.at[s, w, 0, all_rows, lower], u)
        )
        b.wait_recv()
        plus(stage.at[s, w, 2, all_rows, upper], arrived.at[s, w, 2, all_rows, upper])
        live["q", s, w].append(
            go(stage.at[s, w, 2, all_rows, upper], arrived.at[s, w, 1, all_rows, upper], d)
        )

    def finish(s):
        here = pl.ds(s * SLAB, SLAB)
        for w in (1, 0):
            for c in live["q", s, w]:
                c.wait_recv()
            cols = pl.ds(w * wide, wide)
            total = pending[here, cols].astype(f32) + kept[s, w]
            total = total + arrived[s, w, 0].astype(f32) + arrived[s, w, 1].astype(f32)
            updated_ref[here, cols] = total.astype(bf16)

    stages = {
        "product": product, "first": first, "second": second, "across": cross, "norm": norm_back,
        "relay_y": lambda s: relay(s, 0), "relay_z": lambda s: relay(s, 1),
        "sums_y": lambda s: sums(s, 0), "sums_z": lambda s: sums(s, 1),
        "late_y": lambda s: late(s, 0), "late_z": lambda s: late(s, 1), "finish": finish,
    }
    for c in swaps:
        c.wait_recv()
    for name in SUMS:
        stages[name[:-1]](int(name[-1]))
    for c in sends:
        c.wait_send()


def on_device(saved_in, out_grad, pending, gain, alpha, w_query, w_key, w_value, w_out):
    _, rows, depth = saved_in.shape
    width = w_query.shape[2]
    tokens = 16 * rows
    slabs = rows // SLAB
    wide = depth // 2
    vmem = pl.BlockSpec(memory_space=pltpu.VMEM)
    hbm = pl.BlockSpec(memory_space=pltpu.HBM)
    rows_out = pltpu.VMEM((rows, depth), bf16)

    def buffer(*shape):
        return pltpu.VMEM(shape, bf16)

    grad_input, updated = pl.pallas_call(
        kernel,
        out_shape=(rows_out, rows_out),
        in_specs=[hbm] * 9,
        out_specs=(vmem, vmem),
        scratch_shapes=[
            pltpu.SMEM(alpha.shape, f32),
            buffer(rows, depth),
            pltpu.VMEM((1, depth), f32),
            buffer(4, 2, rows, depth),
            buffer(4, 2, rows, depth),
            buffer(2, 3, depth, width),
            buffer(2, width, depth),
            buffer(4, tokens // 2, width),
            buffer(2, 4, tokens // 2, width),
            buffer(tokens, width),
            buffer(tokens, width),
            buffer(tokens, width),
            buffer(tokens, width),
            pltpu.VMEM((tokens, HEAD), f32),
            pltpu.VMEM((tokens, HEAD), f32),
            buffer(2, 3, tokens // 2, width),
            buffer(3, tokens // 2, width),
            buffer(slabs, 4, 2, SLAB, depth),
            buffer(slabs, 2, SLAB, depth),
            buffer(slabs, 2, 2, SLAB, depth),
            buffer(4, SLAB, depth),
            buffer(slabs, SLAB, depth),
            buffer(rows, depth),
            buffer(slabs, 2, 3, SLAB, wide),
            buffer(slabs, 2, 3, SLAB, wide),
            buffer(slabs, 2, 3, SLAB, wide),
            pltpu.VMEM((slabs, 2, SLAB, wide), f32),
            pltpu.SemaphoreType.DMA((43 + 27 * slabs,)),
            pltpu.SemaphoreType.DMA((43 + 27 * slabs,)),
            pltpu.SemaphoreType.DMA((9,)),
        ],
        compiler_params=pltpu.CompilerParams(
            collective_id=1, has_side_effects=True, vmem_limit_bytes=56 * 2**20
        ),
        cost_estimate=pl.CostEstimate(flops=14 * 10**9, bytes_accessed=10**7, transcendentals=10**6),
    )(*(pltpu.with_memory_space_constraint(a, pltpu.HBM) for a in (
        alpha, saved_in[0], gain, out_grad[0], pending[0], w_query[0], w_key[0], w_value[0], w_out[0])))
    return (grad_input[None], updated[None])


def solution(mesh):
    return jax.shard_map(
        on_device,
        mesh=mesh,
        in_specs=(
            P("section", "tp", None),
            P("section", "tp", None),
            P("section", "tp", None),
            P("section", None),
            P(),
            P("section", None, "tp"),
            P("section", None, "tp"),
            P("section", None, "tp"),
            P("section", "tp", None),
        ),
        out_specs=(P("section", "tp", None), P("section", "tp", None)),
        check_vma=False,
    )
```

```python
import math

import jax
import jax.numpy as jnp
from jax import lax
from jax.experimental import pallas as pl
from jax.experimental.pallas import tpu as pltpu
from jax.sharding import PartitionSpec as P

HEAD = 128
SLAB = 16
MESH = pl.DeviceIdType.MESH

eps = 1e-05

f32, bf16 = jnp.float32, jnp.bfloat16

GATHER = (
    "gLlo", "gRlo", "gA", "nrm", "nRhi", "gLhi", "nLlo", "gxR", "nLhi", "nA", "nRlo", "gxL", "gRhi",
    "g3A", "oRlo", "oLhi", "P0t", "P0", "oRhi", "oLlo", "g1A", "G0", "G3", "oxL", "nxR", "oxR",
    "P1t", "g2Ahi", "P3t", "nxL", "P3", "P1", "g2Alo", "G1", "zxR", "zxL", "P2t", "P2", "G2", "S",
)
SUMS = (
    "producta0", "firsta0", "firsta1", "productb0", "firstb0", "firstb1", "product2", "second1",
    "second0", "across1", "across0", "first2", "norm1", "relay_y1", "norm0", "first3", "sums_y1",
    "relay_z1", "relay_y0", "second2", "sums_y0", "relay_z0", "second3", "across2", "across3",
    "sums_z1", "norm2", "norm3", "sums_z0", "relay_z2", "relay_y2", "late_z1", "late_y0",
    "relay_z3", "relay_y3", "sums_y2", "sums_z2", "sums_y3", "late_z0", "sums_z3", "late_y2",
    "late_y1", "late_z2", "late_y3", "finish0", "late_z3", "finish1", "finish2", "finish3",
)
ACROSS_FIRST = (0,)


def dot(a, b, ca, cb):
    return lax.dot_general(a, b, (((ca,), (cb,)), ((), ())), preferred_element_type=f32)


def neighbours():
    place = lax.axis_index("tp")
    x, z, core = place // 4, lax.rem(place // 2, 2), lax.rem(place, 2)
    right = lax.rem(x + 1, 4) * 4 + z * 2 + core
    left = lax.rem(x + 3, 4) * 4 + z * 2 + core
    across = x * 4 + (1 - z) * 2 + core
    twin = x * 4 + z * 2 + (1 - core)
    return x, z, core, {"tp": right}, {"tp": left}, {"tp": across}, {"tp": twin}


def kernel(alpha_in, saved_in, gain_in, grad_ref, pending_ref, wq_ref, wk_ref, wv_ref, wo_ref,
           in_grads_ref, updated_ref,
           alpha_ref, saved_ref, gain_ref, normed, grads, weights, out_weights, theirs, heads,
           q_ref, k_ref, v_ref, g_ref, probs_f, outputs, dk_acc, dv_acc, own_sums,
           back, back_twin, part, xb1, xb2, za, zb,
           pending, gather, stage, arrived, kept,
           send_sem, recv_sem, load_sem):
    x, z, core, right, left, across, twin = neighbours()
    section = lax.axis_index("section")
    y, zh = section // 4, lax.rem(section, 4)
    rows, depth = saved_ref.shape
    width = wq_ref.shape[1]
    pair, half = 2 * rows, rows // 2
    wide = depth // 2
    narrow = wide // 2
    other = 1 - z

    def at(dy, dz):
        return lax.rem(y + dy + 4, 4) * 4 + lax.rem(zh + dz + 4, 4)

    up = ({"section": at(1, 0)}, {"section": at(0, 1)})
    down = ({"section": at(3, 0)}, {"section": at(0, 3)})

    sends, indices, local = [], iter(range(send_sem.shape[0])), iter(range(load_sem.shape[0]))

    def go(src, dst, to):
        index = next(indices)
        c = pltpu.make_async_remote_copy(
            src_ref=src, dst_ref=dst, send_sem=send_sem.at[index], recv_sem=recv_sem.at[index],
            device_id=to, device_id_type=MESH,
        )
        c.start()
        sends.append(c)
        return c

    def move(src, dst):
        c = pltpu.make_async_copy(src, dst, load_sem.at[next(local)])
        c.start()
        return c

    load_rows = [move(saved_in, saved_ref), move(gain_in, gain_ref)]
    own_grads = move(grad_ref, grads.at[0, z])
    loads = [
        move(wq_ref, weights.at[0, 0]),
        move(wk_ref, weights.at[0, 1]),
        move(wv_ref, weights.at[0, 2]),
        move(wo_ref, out_weights.at[0]),
    ]
    load_late = [move(pending_ref, pending), move(alpha_in, alpha_ref)]

    barrier = pltpu.get_barrier_semaphore()
    friends = (right, left, across, twin) + up + down
    for friend in friends:
        pl.semaphore_signal(barrier, inc=1, device_id=friend, device_id_type=MESH)
    pl.semaphore_wait(barrier, len(friends))

    w_twin = []
    lo, hi = pl.ds(0, half), pl.ds(half, half)
    quarter = [pl.ds(i * SLAB, SLAB) for i in range(rows // SLAB)]
    sent = {}

    def normalize():
        for c in load_rows:
            c.wait()

        def one(i, carry):
            here = pl.ds(pl.multiple_of(i * 16, 16), 16)
            values = saved_ref[here, :].astype(f32)
            factor = lax.rsqrt(jnp.mean(values * values, axis=-1, keepdims=True) + eps)
            normed[0, z, here, :] = (values * factor * gain_ref[...]).astype(bf16)
            return carry

        lax.fori_loop(0, rows // 16, one, 0)
        for j, w in enumerate((wq_ref, wk_ref, wv_ref)):
            w_twin.append(go(w, weights.at[1, j], twin))
        w_twin.append(go(wo_ref, out_weights.at[1], twin))

    def place_of(r):
        return pl.ds(pl.multiple_of(lax.rem(x + 4 - r, 4) * pair, pair), pair)

    results = []

    def hand_over(r, first, count):
        js, here = pl.ds(first, count), place_of(r)
        results.append(go(theirs.at[js, here], heads.at[core, js, here], twin))

    def project(r, which):
        if r == 0:
            for c in (w_twin if which else loads)[:3]:
                c.wait_recv() if which else c.wait()
        here = place_of(r)

        def one(j, carry):
            product = dot(normed[r].reshape(pair, depth), weights[which, j], 1, 0).astype(bf16)
            if which == 0:
                heads[core, j, here, :] = product
            else:
                theirs[j, here, :] = product
            return carry

        lax.fori_loop(0, 3, one, 0)
        if which == 1:
            hand_over(r, 0, 3)

    def project_grads(r):
        if r == 0:
            own_grads.wait()
            loads[3].wait()
            w_twin[3].wait_recv()
        here = place_of(r)
        for which in (1, 0):
            product = dot(grads[r].reshape(pair, depth), out_weights[which], 1, 1).astype(bf16)
            if which == 0:
                heads[core, 3, here, :] = product
            else:
                theirs[3, here, :] = product
                hand_over(r, 3, 1)

    mine, crossed = normed.at[0, z], normed.at[0, other]
    moves = {
        "gA": ((), grad_ref, grads.at[0, z], across),
        "nA": ((), mine, mine, across),
        "gxR": (("gRlo",), grads.at[1, z, lo], grads.at[2, z, lo], right),
        "gxL": (("gLhi",), grads.at[3, z, hi], grads.at[2, z, hi], left),
        "nxR": (("nRlo",), normed.at[1, z, lo], normed.at[2, z, lo], right),
        "nxL": (("nLhi",), normed.at[3, z, hi], normed.at[2, z, hi], left),
        "oxR": (("oRlo",), normed.at[1, other, lo], normed.at[2, other, lo], right),
        "oxL": (("oLhi",), normed.at[3, other, hi], normed.at[2, other, hi], left),
        "g1A": (("gRlo", "gRhi"), grads.at[1, z], grads.at[1, z], across),
        "g3A": (("gLlo", "gLhi"), grads.at[3, z], grads.at[3, z], across),
        "g2Alo": (("gxR",), grads.at[2, z, quarter[1]], grads.at[2, z, quarter[1]], across),
        "g2Ahi": (("gxL",), grads.at[2, z, quarter[2]], grads.at[2, z, quarter[2]], across),
        "zxR": (("g1A",), grads.at[1, other, quarter[0]], grads.at[2, other, quarter[0]], right),
        "zxL": (("g3A",), grads.at[3, other, quarter[3]], grads.at[2, other, quarter[3]], left),
    }
    for end, part_rows in (("lo", lo), ("hi", hi)):
        for way, r, to in (("R", 1, right), ("L", 3, left)):
            moves["g" + way + end] = ((), grad_ref.at[part_rows], grads.at[r, z, part_rows], to)
            moves["n" + way + end] = ((), mine.at[part_rows], normed.at[r, z, part_rows], to)
            moves["o" + way + end] = (("nA",), crossed.at[part_rows], normed.at[r, other, part_rows], to)
    needs = {
        "P0": ("nA",), "P1": ("nRlo", "nRhi", "oRlo", "oRhi"), "P3": ("nLlo", "nLhi", "oLlo", "oLhi"),
        "P2": ("nxR", "nxL", "oxR", "oxL"), "G0": ("gA",), "G1": ("gRlo", "gRhi", "g1A"),
        "G3": ("gLlo", "gLhi", "g3A"), "G2": ("gxR", "gxL", "g2Alo", "g2Ahi", "zxR", "zxL"),
    }
    tokens = q_ref.shape[0]
    block = 512
    chips = tokens // pair
    scale = 1.0 / math.sqrt(HEAD)
    places = [(chip, c) for chip in range(chips) for c in (0, 1)]
    below = lax.broadcasted_iota(jnp.int32, (block, block), 0) <= lax.broadcasted_iota(
        jnp.int32, (block, block), 1
    )

    def assemble(j, ref):
        for chip, c in places:
            ref[pl.ds((2 * chip + c) * rows, rows), :] = heads[c, j, pl.ds(chip * rows, rows), :]

    def take_scores():
        for c in results:
            c.wait_recv()
        results.clear()
        for j, ref in enumerate((q_ref, k_ref, v_ref)):
            assemble(j, ref)
        for head in range(width // HEAD):
            cols = pl.ds(head * HEAD, HEAD)
            values_t = v_ref[:, cols].T
            for step in reversed(range(tokens // block)):
                n = (step + 1) * block
                mine_rows = pl.ds(step * block, block)
                scores = dot(k_ref[pl.ds(0, n), cols], q_ref[mine_rows, cols], 1, 1)
                scores = scores * (scale * math.log2(math.e))
                last = jnp.where(below, scores[n - block :], -1e30)
                scores = last if step == 0 else jnp.concatenate((scores[: n - block], last), axis=0)
                exps = jnp.exp2(scores - jnp.max(scores, axis=0, keepdims=True))
                exps = exps * (1.0 / jnp.sum(exps, axis=0, keepdims=True))
                probs_f[head, pl.ds(0, n), mine_rows] = exps
                outputs[head, :, mine_rows] = dot(values_t[:, :n], exps.astype(bf16), 1, 0)

    landed = set()

    def need(names):
        for name in names:
            if name not in landed:
                landed.add(name)
                sent[name].wait_recv()

    for name in GATHER:
        if name == "nrm":
            normalize()
        elif name == "S":
            take_scores()
        elif name in moves:
            waits, src, dst, to = moves[name]
            need(waits)
            sent[name] = go(src, dst, to)
        else:
            need(needs[name[:2]])
            if name[0] == "P":
                project(int(name[1]), 1 if name.endswith("t") else 0)
            else:
                project_grads(int(name[1]))
    for c in results:
        c.wait_recv()

    assemble(3, g_ref)

    def put(j, chip, c, cols, value):
        for s in range(rows // SLAB):
            there = pl.ds((s * chips + chip) * SLAB, SLAB)
            back[c, j, there, cols] = value[s * SLAB : (s + 1) * SLAB].astype(bf16)

    swaps = []
    for head in range(width // HEAD):
        cols = pl.ds(head * HEAD, HEAD)
        keys_t = k_ref[:, cols].T
        for step in reversed(range(tokens // block)):
            n = (step + 1) * block
            mine_rows = pl.ds(step * block, block)
            query, grad = q_ref[mine_rows, cols], g_ref[mine_rows, cols]
            delta = jnp.sum(grad.astype(f32).T * outputs[head, :, mine_rows], axis=0, keepdims=True)
            grad_probs = dot(v_ref[pl.ds(0, n), cols], grad, 1, 1)
            exps = probs_f[head, pl.ds(0, n), mine_rows]
            grad_scores = (exps * ((grad_probs - delta) * scale)).astype(bf16)
            grad_query = dot(keys_t[:, :n], grad_scores, 1, 0).T
            for chip, c in places:
                offset = (2 * chip + c) * rows - step * block
                if 0 <= offset < block:
                    put(0, chip, c, cols, grad_query[offset : offset + rows])
            more_k = dot(grad_scores, query, 1, 0)
            more_v = dot(exps.astype(bf16), grad, 1, 0)
            if step == tokens // block - 1:
                dk_acc[...] = more_k
                dv_acc[...] = more_v
            else:
                dk_acc[pl.ds(0, n)] += more_k
                dv_acc[pl.ds(0, n)] += more_v
        for j, acc in ((1, dk_acc), (2, dv_acc)):
            for chip, c in places:
                put(j, chip, c, cols, acc[pl.ds((2 * chip + c) * rows, rows), :])
        everything = pl.ds(0, tokens // 2)
        swaps.append(go(back.at[1 - core, :, everything, cols], back_twin.at[:, everything, cols], twin))

    slabs = rows // SLAB
    all_rows = pl.ds(0, SLAB)
    chunk = 512
    together = chips * SLAB

    def coefficient(j, s):
        return jnp.where(s > j, alpha_ref[s, j], 0.0)

    for c in load_late:
        c.wait()
    coeffs = {}
    for r in range(4):
        for t in range(4):
            coeffs[0, r, t] = coefficient(at(0, r), at(4 - t, 0))
            coeffs[1, r, t] = coefficient(at(r, 0), at(0, 4 - t))

    def spot(r):
        return lax.rem(x + r, 4)

    def plus(target, source):
        target[...] = (target[...].astype(f32) + source[...].astype(f32)).astype(bf16)

    live = {}

    def partial(j, s, n, lefts):
        here = pl.ds(s * together, 2 * together)
        cols = pl.ds(pl.multiple_of(n * chunk, chunk), chunk)
        total = dot(lefts[0, here, :], weights[j, 0, cols, :], 1, 1)
        for k in (1, 2):
            total += dot(lefts[k, here, :], weights[j, k, cols, :], 1, 1)
        return total

    def store(s, n, total):
        cols = pl.ds(pl.multiple_of(n * chunk, chunk), chunk)
        part[s : s + 2, :, :, :, cols] = total.astype(bf16).reshape(2, chips // 2, 2, SLAB, chunk)

    def product(s, begin=0):
        def step(n, carry):
            store(s, n, partial(0, s, n, back.at[core]) + partial(1, s, n, back_twin))
            return carry

        lax.fori_loop(begin, depth // chunk, step, 0)

    def own_half():
        def step(n, carry):
            own_sums[n] = partial(0, 0, n, back.at[core])
            return carry

        lax.fori_loop(0, 3, step, 0)

    def first_half(s):
        def step(n, carry):
            store(s, n, own_sums[n] + partial(1, s, n, back_twin))
            return carry

        lax.fori_loop(0, 3, step, 0)

    early, latter = pl.ds(0, wide), pl.ds(wide, wide)

    whole = pl.ds(0, depth)

    def first(s, cols):
        def lay(key, src, dst, to):
            live.setdefault(key, []).append(go(src.at[all_rows, cols], dst.at[all_rows, cols], to))

        if s in ACROSS_FIRST:
            for r in (2, 1, 3, 0):
                lay(("za", s, r), part.at[s, spot(r), other], za.at[r], across)
            return
        lay(("x1r", s), part.at[s, spot(2), 0], xb1.at[s, 0], right)
        lay(("x1l", s), part.at[s, spot(2), 1], xb1.at[s, 1], left)
        lay(("x2", s), part.at[s, spot(1), 1], xb2.at[s, 0, 1], right)
        lay(("x2", s), part.at[s, spot(3), 0], xb2.at[s, 1, 0], left)

    def arrive(*key):
        for c in live[key]:
            c.wait_recv()

    def second(s):
        if s in ACROSS_FIRST:
            two, one, three = (part.at[s, spot(r), z] for r in (2, 1, 3))
            arrive("za", s, 2)
            plus(two, za.at[2])
            live["x1r", s] = [go(two.at[all_rows, early], xb1.at[s, 0, all_rows, early], right)]
            live["x1l", s] = [go(two.at[all_rows, latter], xb1.at[s, 0, all_rows, latter], left)]
            arrive("za", s, 1)
            plus(one, za.at[1])
            live["x2", s] = [go(one.at[all_rows, latter], xb2.at[s, 0, 0, all_rows, latter], right)]
            arrive("za", s, 3)
            plus(three, za.at[3])
            live["x2", s].append(go(three.at[all_rows, early], xb2.at[s, 1, 0, all_rows, early], left))
            return
        arrive("x1r", s)
        plus(part.at[s, spot(1), 0], xb1.at[s, 0])
        live["x2", s].append(go(part.at[s, spot(1), 0], xb2.at[s, 0, 0], right))
        arrive("x1l", s)
        plus(part.at[s, spot(3), 1], xb1.at[s, 1])
        live["x2", s].append(go(part.at[s, spot(3), 1], xb2.at[s, 1, 1], left))

    def cross(s):
        if s in ACROSS_FIRST:
            one, three = (part.at[s, spot(r), z] for r in (1, 3))
            arrive("x1r", s)
            plus(one.at[all_rows, early], xb1.at[s, 0, all_rows, early])
            live["x2", s].append(go(one.at[all_rows, early], xb2.at[s, 0, 0, all_rows, early], right))
            arrive("x1l", s)
            plus(three.at[all_rows, latter], xb1.at[s, 0, all_rows, latter])
            live["x2", s].append(go(three.at[all_rows, latter], xb2.at[s, 1, 0, all_rows, latter], left))
            return
        for c in live["x2", s]:
            c.wait_recv()
        total = part[s, x, other].astype(f32) + xb2[s, 0, other].astype(f32) + xb2[s, 1, other].astype(f32)
        part[s, x, other] = total.astype(bf16)
        live["z", s] = go(part.at[s, x, other], zb.at[s], across)

    def norm_back(s):
        here = pl.ds(s * SLAB, SLAB)
        if s in ACROSS_FIRST:
            arrive("x2", s)
            arrive("za", s, 0)
        else:
            live["z", s].wait_recv()
        saved = saved_ref[here, :].astype(f32)
        last, k = (za[0], 0) if s in ACROSS_FIRST else (zb[s], z)
        total = part[s, x, z].astype(f32) + xb2[s, 0, k].astype(f32)
        total = total + xb2[s, 1, k].astype(f32) + last.astype(f32)
        factor = lax.rsqrt(jnp.mean(saved * saved, axis=-1, keepdims=True) + eps)
        scaled = total * gain_ref[...]
        inner = jnp.mean(scaled * saved, axis=-1, keepdims=True)
        change = factor * (scaled - saved * (factor * factor * inner))
        value = (grads[0, z, here, :].astype(f32) + change).astype(bf16)
        in_grads_ref[here, :] = value
        for w in (0, 1):
            source = in_grads_ref.at[here, pl.ds(w * wide, wide)]
            live["g", s, w] = (
                go(source, gather.at[s, w, 0], up[w]),
                go(source, gather.at[s, w, 2], down[w]),
            )

    lower, upper = pl.ds(0, narrow), pl.ds(narrow, narrow)

    def relay(s, w):
        one, three = live["g", s, w]
        one.wait_recv()
        a = go(gather.at[s, w, 0, all_rows, lower], gather.at[s, w, 1, all_rows, lower], up[w])
        three.wait_recv()
        b = go(gather.at[s, w, 2, all_rows, upper], gather.at[s, w, 1, all_rows, upper], down[w])
        live["r", s, w] = (a, b)

    def sums(s, w):
        for c in live["r", s, w]:
            c.wait_recv()

        def body(i, carry):
            cols = pl.ds(pl.multiple_of(i * 256, 256), 256)
            own = pl.ds(pl.multiple_of(w * wide + i * 256, 256), 256)
            blocks = [in_grads_ref[pl.ds(s * SLAB, SLAB), own].astype(f32)]
            blocks += [gather[s, w, t, :, cols].astype(f32) for t in range(3)]
            for r in range(4):
                total = blocks[0] * coeffs[w, r, 0]
                for t in (1, 2, 3):
                    total = total + blocks[t] * coeffs[w, r, t]
                if r == 0:
                    kept[s, w, :, cols] = total
                else:
                    stage[s, w, r - 1, :, cols] = total.astype(bf16)
            return carry

        lax.fori_loop(0, wide // 256, body, 0)
        u, d = up[1 - w], down[1 - w]
        live["p", s, w] = (
            go(stage.at[s, w, 1, all_rows, lower], arrived.at[s, w, 2, all_rows, lower], u),
            go(stage.at[s, w, 1, all_rows, upper], arrived.at[s, w, 2, all_rows, upper], d),
        )
        live["q", s, w] = [
            go(stage.at[s, w, 0, all_rows, upper], arrived.at[s, w, 0, all_rows, upper], u),
            go(stage.at[s, w, 2, all_rows, lower], arrived.at[s, w, 1, all_rows, lower], d),
        ]

    def late(s, w):
        a, b = live["p", s, w]
        u, d = up[1 - w], down[1 - w]
        a.wait_recv()
        plus(stage.at[s, w, 0, all_rows, lower], arrived.at[s, w, 2, all_rows, lower])
        live["q", s, w].append(
            go(stage.at[s, w, 0, all_rows, lower], arrived.at[s, w, 0, all_rows, lower], u)
        )
        b.wait_recv()
        plus(stage.at[s, w, 2, all_rows, upper], arrived.at[s, w, 2, all_rows, upper])
        live["q", s, w].append(
            go(stage.at[s, w, 2, all_rows, upper], arrived.at[s, w, 1, all_rows, upper], d)
        )

    def finish(s):
        here = pl.ds(s * SLAB, SLAB)
        for w in (1, 0):
            for c in live["q", s, w]:
                c.wait_recv()
            cols = pl.ds(w * wide, wide)
            total = pending[here, cols].astype(f32) + kept[s, w]
            total = total + arrived[s, w, 0].astype(f32) + arrived[s, w, 1].astype(f32)
            updated_ref[here, cols] = total.astype(bf16)

    stages = {
        "product": product, "producta": first_half, "productb": lambda s: product(s, 3),
        "first": lambda s: first(s, whole), "firsta": lambda s: first(s, early),
        "firstb": lambda s: first(s, latter), "second": second, "across": cross, "norm": norm_back,
        "relay_y": lambda s: relay(s, 0), "relay_z": lambda s: relay(s, 1),
        "sums_y": lambda s: sums(s, 0), "sums_z": lambda s: sums(s, 1),
        "late_y": lambda s: late(s, 0), "late_z": lambda s: late(s, 1), "finish": finish,
    }
    own_half()
    for c in swaps:
        c.wait_recv()
    for name in SUMS:
        stages[name[:-1]](int(name[-1]))
    for c in sends:
        c.wait_send()


def on_device(saved_in, out_grad, pending, gain, alpha, w_query, w_key, w_value, w_out):
    _, rows, depth = saved_in.shape
    width = w_query.shape[2]
    tokens = 16 * rows
    slabs = rows // SLAB
    wide = depth // 2
    vmem = pl.BlockSpec(memory_space=pltpu.VMEM)
    hbm = pl.BlockSpec(memory_space=pltpu.HBM)
    rows_out = pltpu.VMEM((rows, depth), bf16)

    def buffer(*shape):
        return pltpu.VMEM(shape, bf16)

    grad_input, updated = pl.pallas_call(
        kernel,
        out_shape=(rows_out, rows_out),
        in_specs=[hbm] * 9,
        out_specs=(vmem, vmem),
        scratch_shapes=[
            pltpu.SMEM(alpha.shape, f32),
            buffer(rows, depth),
            pltpu.VMEM((1, depth), f32),
            buffer(4, 2, rows, depth),
            buffer(4, 2, rows, depth),
            buffer(2, 3, depth, width),
            buffer(2, width, depth),
            buffer(4, tokens // 2, width),
            buffer(2, 4, tokens // 2, width),
            buffer(tokens, width),
            buffer(tokens, width),
            buffer(tokens, width),
            buffer(tokens, width),
            pltpu.VMEM((width // HEAD, tokens, tokens), f32),
            pltpu.VMEM((width // HEAD, HEAD, tokens), f32),
            pltpu.VMEM((tokens, HEAD), f32),
            pltpu.VMEM((tokens, HEAD), f32),
            pltpu.VMEM((3, 4 * rows, 512), f32),
            buffer(2, 3, tokens // 2, width),
            buffer(3, tokens // 2, width),
            buffer(slabs, 4, 2, SLAB, depth),
            buffer(slabs, 2, SLAB, depth),
            buffer(slabs, 2, 2, SLAB, depth),
            buffer(4, SLAB, depth),
            buffer(slabs, SLAB, depth),
            buffer(rows, depth),
            buffer(slabs, 2, 3, SLAB, wide),
            buffer(slabs, 2, 3, SLAB, wide),
            buffer(slabs, 2, 3, SLAB, wide),
            pltpu.VMEM((slabs, 2, SLAB, wide), f32),
            pltpu.SemaphoreType.DMA((48 + 28 * slabs,)),
            pltpu.SemaphoreType.DMA((48 + 28 * slabs,)),
            pltpu.SemaphoreType.DMA((9,)),
        ],
        compiler_params=pltpu.CompilerParams(
            collective_id=1, has_side_effects=True, vmem_limit_bytes=59 * 2**20
        ),
        cost_estimate=pl.CostEstimate(flops=14 * 10**9, bytes_accessed=10**7, transcendentals=10**6),
    )(*(pltpu.with_memory_space_constraint(a, pltpu.HBM) for a in (
        alpha, saved_in[0], gain, out_grad[0], pending[0], w_query[0], w_key[0], w_value[0], w_out[0])))
    return (grad_input[None], updated[None])


def solution(mesh):
    return jax.shard_map(
        on_device,
        mesh=mesh,
        in_specs=(
            P("section", "tp", None),
            P("section", "tp", None),
            P("section", "tp", None),
            P("section", None),
            P(),
            P("section", None, "tp"),
            P("section", None, "tp"),
            P("section", None, "tp"),
            P("section", "tp", None),
        ),
        out_specs=(P("section", "tp", None), P("section", "tp", None)),
        check_vma=False,
    )
```

```python
import math

import jax
import jax.numpy as jnp
from jax import lax
from jax.experimental import pallas as pl
from jax.experimental.pallas import tpu as pltpu
from jax.sharding import PartitionSpec as P

HEAD = 128
SLAB = 16
MESH = pl.DeviceIdType.MESH

eps = 1e-05

f32, bf16 = jnp.float32, jnp.bfloat16

GATHER = (
    "gLlo", "gRlo", "gA", "nrm", "nRhi", "gLhi", "nLlo", "gxR", "nLhi", "nA", "nRlo", "gxL", "gRhi",
    "g3A", "oRlo", "oLhi", "P0t", "P0", "oRhi", "oLlo", "g1A", "G0", "G3", "oxL", "nxR", "oxR",
    "P1t", "g2Ahi", "P3t", "nxL", "P3", "P1", "g2Alo", "G1", "zxR", "zxL", "P2t", "P2", "S", "G2",
)
SUMS = (
    "producta0", "firsta1", "firsta0", "productb0", "firstb0", "firstb1", "product2", "second1",
    "across1", "second0", "across0", "norm1", "first2", "norm0", "relay_z1", "relay_y1", "first3",
    "relay_y0", "sums_y1", "second2", "relay_z0", "sums_z1", "sums_y0", "second3", "across2",
    "sums_z0", "late_z1", "across3", "norm2", "late_z0", "norm3", "relay_z2", "relay_y3",
    "relay_y2", "late_y1", "relay_z3", "sums_y3", "sums_z2", "sums_y2", "sums_z3", "finish1",
    "late_y3", "late_y0", "late_z2", "late_y2", "late_z3", "finish0", "finish3", "finish2",
)
ACROSS_FIRST = (0,)


def dot(a, b, ca, cb):
    return lax.dot_general(a, b, (((ca,), (cb,)), ((), ())), preferred_element_type=f32)


def neighbours():
    place = lax.axis_index("tp")
    x, z, core = place // 4, lax.rem(place // 2, 2), lax.rem(place, 2)
    right = lax.rem(x + 1, 4) * 4 + z * 2 + core
    left = lax.rem(x + 3, 4) * 4 + z * 2 + core
    across = x * 4 + (1 - z) * 2 + core
    twin = x * 4 + z * 2 + (1 - core)
    return x, z, core, {"tp": right}, {"tp": left}, {"tp": across}, {"tp": twin}


def kernel(alpha_in, saved_in, gain_in, grad_ref, pending_ref, wq_ref, wk_ref, wv_ref, wo_ref,
           in_grads_ref, updated_ref,
           alpha_ref, saved_ref, gain_ref, normed, grads, weights, out_weights, theirs, heads,
           q_ref, k_ref, v_ref, g_ref, probs_f, outputs, dk_acc, dv_acc, own_sums,
           back, back_twin, part, xb1, xb2, za, zb,
           pending, gather, stage, arrived, kept,
           send_sem, recv_sem, load_sem):
    x, z, core, right, left, across, twin = neighbours()
    section = lax.axis_index("section")
    y, zh = section // 4, lax.rem(section, 4)
    rows, depth = saved_ref.shape
    width = wq_ref.shape[1]
    pair, half = 2 * rows, rows // 2
    wide = depth // 2
    narrow = wide // 2
    other = 1 - z

    def at(dy, dz):
        return lax.rem(y + dy + 4, 4) * 4 + lax.rem(zh + dz + 4, 4)

    up = ({"section": at(1, 0)}, {"section": at(0, 1)})
    down = ({"section": at(3, 0)}, {"section": at(0, 3)})

    sends, indices, local = [], iter(range(send_sem.shape[0])), iter(range(load_sem.shape[0]))

    def go(src, dst, to):
        index = next(indices)
        c = pltpu.make_async_remote_copy(
            src_ref=src, dst_ref=dst, send_sem=send_sem.at[index], recv_sem=recv_sem.at[index],
            device_id=to, device_id_type=MESH,
        )
        c.start()
        sends.append(c)
        return c

    def move(src, dst):
        c = pltpu.make_async_copy(src, dst, load_sem.at[next(local)])
        c.start()
        return c

    load_rows = [move(saved_in, saved_ref), move(gain_in, gain_ref)]
    own_grads = move(grad_ref, grads.at[0, z])
    loads = [
        move(wq_ref, weights.at[0, 0]),
        move(wk_ref, weights.at[0, 1]),
        move(wv_ref, weights.at[0, 2]),
        move(wo_ref, out_weights.at[0]),
    ]
    load_late = [move(pending_ref, pending), move(alpha_in, alpha_ref)]

    barrier = pltpu.get_barrier_semaphore()
    friends = (right, left, across, twin) + up + down
    for friend in friends:
        pl.semaphore_signal(barrier, inc=1, device_id=friend, device_id_type=MESH)
    pl.semaphore_wait(barrier, len(friends))

    w_twin = []
    lo, hi = pl.ds(0, half), pl.ds(half, half)
    quarter = [pl.ds(i * SLAB, SLAB) for i in range(rows // SLAB)]
    sent = {}

    def normalize():
        for c in load_rows:
            c.wait()

        def one(i, carry):
            here = pl.ds(pl.multiple_of(i * 16, 16), 16)
            values = saved_ref[here, :].astype(f32)
            factor = lax.rsqrt(jnp.mean(values * values, axis=-1, keepdims=True) + eps)
            normed[0, z, here, :] = (values * factor * gain_ref[...]).astype(bf16)
            return carry

        lax.fori_loop(0, rows // 16, one, 0)
        for j, w in enumerate((wq_ref, wk_ref, wv_ref)):
            w_twin.append(go(w, weights.at[1, j], twin))
        w_twin.append(go(wo_ref, out_weights.at[1], twin))

    def place_of(r):
        return pl.ds(pl.multiple_of(lax.rem(x + 4 - r, 4) * pair, pair), pair)

    results = []

    def hand_over(r, first, count):
        js, here = pl.ds(first, count), place_of(r)
        results.append(go(theirs.at[js, here], heads.at[core, js, here], twin))

    def project(r, which):
        if r == 0:
            for c in (w_twin if which else loads)[:3]:
                c.wait_recv() if which else c.wait()
        here = place_of(r)

        def one(j, carry):
            product = dot(normed[r].reshape(pair, depth), weights[which, j], 1, 0).astype(bf16)
            if which == 0:
                heads[core, j, here, :] = product
            else:
                theirs[j, here, :] = product
            return carry

        lax.fori_loop(0, 3, one, 0)
        if which == 1:
            hand_over(r, 0, 3)

    def project_grads(r):
        if r == 0:
            own_grads.wait()
            loads[3].wait()
            w_twin[3].wait_recv()
        here = place_of(r)
        for which in (1, 0):
            product = dot(grads[r].reshape(pair, depth), out_weights[which], 1, 1).astype(bf16)
            if which == 0:
                heads[core, 3, here, :] = product
            else:
                theirs[3, here, :] = product
                hand_over(r, 3, 1)

    mine, crossed = normed.at[0, z], normed.at[0, other]
    moves = {
        "gA": ((), grad_ref, grads.at[0, z], across),
        "nA": ((), mine, mine, across),
        "gxR": (("gRlo",), grads.at[1, z, lo], grads.at[2, z, lo], right),
        "gxL": (("gLhi",), grads.at[3, z, hi], grads.at[2, z, hi], left),
        "nxR": (("nRlo",), normed.at[1, z, lo], normed.at[2, z, lo], right),
        "nxL": (("nLhi",), normed.at[3, z, hi], normed.at[2, z, hi], left),
        "oxR": (("oRlo",), normed.at[1, other, lo], normed.at[2, other, lo], right),
        "oxL": (("oLhi",), normed.at[3, other, hi], normed.at[2, other, hi], left),
        "g1A": (("gRlo", "gRhi"), grads.at[1, z], grads.at[1, z], across),
        "g3A": (("gLlo", "gLhi"), grads.at[3, z], grads.at[3, z], across),
        "g2Alo": (("gxR",), grads.at[2, z, quarter[1]], grads.at[2, z, quarter[1]], across),
        "g2Ahi": (("gxL",), grads.at[2, z, quarter[2]], grads.at[2, z, quarter[2]], across),
        "zxR": (("g1A",), grads.at[1, other, quarter[0]], grads.at[2, other, quarter[0]], right),
        "zxL": (("g3A",), grads.at[3, other, quarter[3]], grads.at[2, other, quarter[3]], left),
    }
    for end, part_rows in (("lo", lo), ("hi", hi)):
        for way, r, to in (("R", 1, right), ("L", 3, left)):
            moves["g" + way + end] = ((), grad_ref.at[part_rows], grads.at[r, z, part_rows], to)
            moves["n" + way + end] = ((), mine.at[part_rows], normed.at[r, z, part_rows], to)
            moves["o" + way + end] = (("nA",), crossed.at[part_rows], normed.at[r, other, part_rows], to)
    needs = {
        "P0": ("nA",), "P1": ("nRlo", "nRhi", "oRlo", "oRhi"), "P3": ("nLlo", "nLhi", "oLlo", "oLhi"),
        "P2": ("nxR", "nxL", "oxR", "oxL"), "G0": ("gA",), "G1": ("gRlo", "gRhi", "g1A"),
        "G3": ("gLlo", "gLhi", "g3A"), "G2": ("gxR", "gxL", "g2Alo", "g2Ahi", "zxR", "zxL"),
    }
    tokens = q_ref.shape[0]
    block = 512
    chips = tokens // pair
    scale = 1.0 / math.sqrt(HEAD)
    places = [(chip, c) for chip in range(chips) for c in (0, 1)]
    below = lax.broadcasted_iota(jnp.int32, (block, block), 0) <= lax.broadcasted_iota(
        jnp.int32, (block, block), 1
    )

    def assemble(j, ref):
        for chip, c in places:
            ref[pl.ds((2 * chip + c) * rows, rows), :] = heads[c, j, pl.ds(chip * rows, rows), :]

    def take_scores():
        for c in results:
            c.wait_recv()
        results.clear()
        for j, ref in enumerate((q_ref, k_ref, v_ref)):
            assemble(j, ref)
        for head in range(width // HEAD):
            cols = pl.ds(head * HEAD, HEAD)
            values_t = v_ref[:, cols].T
            for step in reversed(range(tokens // block)):
                n = (step + 1) * block
                mine_rows = pl.ds(step * block, block)
                scores = dot(k_ref[pl.ds(0, n), cols], q_ref[mine_rows, cols], 1, 1)
                scores = scores * (scale * math.log2(math.e))
                last = jnp.where(below, scores[n - block :], -1e30)
                scores = last if step == 0 else jnp.concatenate((scores[: n - block], last), axis=0)
                exps = jnp.exp2(scores - jnp.max(scores, axis=0, keepdims=True))
                exps = exps * (1.0 / jnp.sum(exps, axis=0, keepdims=True))
                probs_f[head, pl.ds(0, n), mine_rows] = exps
                outputs[head, :, mine_rows] = dot(values_t[:, :n], exps.astype(bf16), 1, 0)

    landed = set()

    def need(names):
        for name in names:
            if name not in landed:
                landed.add(name)
                sent[name].wait_recv()

    for name in GATHER:
        if name == "nrm":
            normalize()
        elif name == "S":
            take_scores()
        elif name in moves:
            waits, src, dst, to = moves[name]
            need(waits)
            sent[name] = go(src, dst, to)
        else:
            need(needs[name[:2]])
            if name[0] == "P":
                project(int(name[1]), 1 if name.endswith("t") else 0)
            else:
                project_grads(int(name[1]))
    for c in results:
        c.wait_recv()

    assemble(3, g_ref)

    def put(j, chip, c, cols, value):
        for s in range(rows // SLAB):
            there = pl.ds((s * chips + chip) * SLAB, SLAB)
            back[c, j, there, cols] = value[s * SLAB : (s + 1) * SLAB].astype(bf16)

    swaps = []
    for head in range(width // HEAD):
        cols = pl.ds(head * HEAD, HEAD)
        keys_t = k_ref[:, cols].T
        for step in reversed(range(tokens // block)):
            n = (step + 1) * block
            mine_rows = pl.ds(step * block, block)
            query, grad = q_ref[mine_rows, cols], g_ref[mine_rows, cols]
            delta = jnp.sum(grad.astype(f32).T * outputs[head, :, mine_rows], axis=0, keepdims=True)
            grad_probs = dot(v_ref[pl.ds(0, n), cols], grad, 1, 1)
            exps = probs_f[head, pl.ds(0, n), mine_rows]
            grad_scores = (exps * ((grad_probs - delta) * scale)).astype(bf16)
            grad_query = dot(keys_t[:, :n], grad_scores, 1, 0).T
            for chip, c in places:
                offset = (2 * chip + c) * rows - step * block
                if 0 <= offset < block:
                    put(0, chip, c, cols, grad_query[offset : offset + rows])
            more_k = dot(grad_scores, query, 1, 0)
            more_v = dot(exps.astype(bf16), grad, 1, 0)
            if step == tokens // block - 1:
                dk_acc[...] = more_k
                dv_acc[...] = more_v
            else:
                dk_acc[pl.ds(0, n)] += more_k
                dv_acc[pl.ds(0, n)] += more_v
        for j, acc in ((1, dk_acc), (2, dv_acc)):
            for chip, c in places:
                put(j, chip, c, cols, acc[pl.ds((2 * chip + c) * rows, rows), :])
        everything = pl.ds(0, tokens // 2)
        swaps.append(go(back.at[1 - core, :, everything, cols], back_twin.at[:, everything, cols], twin))

    slabs = rows // SLAB
    all_rows = pl.ds(0, SLAB)
    chunk = 512
    together = chips * SLAB

    def coefficient(j, s):
        return jnp.where(s > j, alpha_ref[s, j], 0.0)

    for c in load_late:
        c.wait()
    coeffs = {}
    for r in range(4):
        for t in range(4):
            coeffs[0, r, t] = coefficient(at(0, r), at(4 - t, 0))
            coeffs[1, r, t] = coefficient(at(r, 0), at(0, 4 - t))

    def spot(r):
        return lax.rem(x + r, 4)

    def plus(target, source):
        target[...] = (target[...].astype(f32) + source[...].astype(f32)).astype(bf16)

    live = {}

    def partial(j, s, n, lefts):
        here = pl.ds(s * together, 2 * together)
        cols = pl.ds(pl.multiple_of(n * chunk, chunk), chunk)
        total = dot(lefts[0, here, :], weights[j, 0, cols, :], 1, 1)
        for k in (1, 2):
            total += dot(lefts[k, here, :], weights[j, k, cols, :], 1, 1)
        return total

    def store(s, n, total):
        cols = pl.ds(pl.multiple_of(n * chunk, chunk), chunk)
        part[s : s + 2, :, :, :, cols] = total.astype(bf16).reshape(2, chips // 2, 2, SLAB, chunk)

    def product(s, begin=0):
        def step(n, carry):
            store(s, n, partial(0, s, n, back.at[core]) + partial(1, s, n, back_twin))
            return carry

        lax.fori_loop(begin, depth // chunk, step, 0)

    def own_half():
        def step(n, carry):
            own_sums[n] = partial(0, 0, n, back.at[core])
            return carry

        lax.fori_loop(0, 3, step, 0)

    def first_half(s):
        def step(n, carry):
            store(s, n, own_sums[n] + partial(1, s, n, back_twin))
            return carry

        lax.fori_loop(0, 3, step, 0)

    early, latter = pl.ds(0, wide), pl.ds(wide, wide)

    whole = pl.ds(0, depth)

    def first(s, cols):
        def lay(key, src, dst, to):
            live.setdefault(key, []).append(go(src.at[all_rows, cols], dst.at[all_rows, cols], to))

        if s in ACROSS_FIRST:
            for r in (2, 1, 3, 0):
                lay(("za", s, r), part.at[s, spot(r), other], za.at[r], across)
            return
        lay(("x1r", s), part.at[s, spot(2), 0], xb1.at[s, 0], right)
        lay(("x1l", s), part.at[s, spot(2), 1], xb1.at[s, 1], left)
        lay(("x2", s), part.at[s, spot(1), 1], xb2.at[s, 0, 1], right)
        lay(("x2", s), part.at[s, spot(3), 0], xb2.at[s, 1, 0], left)

    def arrive(*key):
        for c in live[key]:
            c.wait_recv()

    def second(s):
        if s in ACROSS_FIRST:
            two, one, three = (part.at[s, spot(r), z] for r in (2, 1, 3))
            arrive("za", s, 2)
            plus(two, za.at[2])
            live["x1r", s] = [go(two.at[all_rows, early], xb1.at[s, 0, all_rows, early], right)]
            live["x1l", s] = [go(two.at[all_rows, latter], xb1.at[s, 0, all_rows, latter], left)]
            arrive("za", s, 1)
            plus(one, za.at[1])
            live["x2", s] = [go(one.at[all_rows, latter], xb2.at[s, 0, 0, all_rows, latter], right)]
            arrive("za", s, 3)
            plus(three, za.at[3])
            live["x2", s].append(go(three.at[all_rows, early], xb2.at[s, 1, 0, all_rows, early], left))
            return
        arrive("x1r", s)
        plus(part.at[s, spot(1), 0], xb1.at[s, 0])
        live["x2", s].append(go(part.at[s, spot(1), 0], xb2.at[s, 0, 0], right))
        arrive("x1l", s)
        plus(part.at[s, spot(3), 1], xb1.at[s, 1])
        live["x2", s].append(go(part.at[s, spot(3), 1], xb2.at[s, 1, 1], left))

    def cross(s):
        if s in ACROSS_FIRST:
            one, three = (part.at[s, spot(r), z] for r in (1, 3))
            arrive("x1r", s)
            plus(one.at[all_rows, early], xb1.at[s, 0, all_rows, early])
            live["x2", s].append(go(one.at[all_rows, early], xb2.at[s, 0, 0, all_rows, early], right))
            arrive("x1l", s)
            plus(three.at[all_rows, latter], xb1.at[s, 0, all_rows, latter])
            live["x2", s].append(go(three.at[all_rows, latter], xb2.at[s, 1, 0, all_rows, latter], left))
            return
        for c in live["x2", s]:
            c.wait_recv()
        total = part[s, x, other].astype(f32) + xb2[s, 0, other].astype(f32) + xb2[s, 1, other].astype(f32)
        part[s, x, other] = total.astype(bf16)
        live["z", s] = go(part.at[s, x, other], zb.at[s], across)

    def norm_back(s):
        here = pl.ds(s * SLAB, SLAB)
        if s in ACROSS_FIRST:
            arrive("x2", s)
            arrive("za", s, 0)
        else:
            live["z", s].wait_recv()
        saved = saved_ref[here, :].astype(f32)
        last, k = (za[0], 0) if s in ACROSS_FIRST else (zb[s], z)
        total = part[s, x, z].astype(f32) + xb2[s, 0, k].astype(f32)
        total = total + xb2[s, 1, k].astype(f32) + last.astype(f32)
        factor = lax.rsqrt(jnp.mean(saved * saved, axis=-1, keepdims=True) + eps)
        scaled = total * gain_ref[...]
        inner = jnp.mean(scaled * saved, axis=-1, keepdims=True)
        change = factor * (scaled - saved * (factor * factor * inner))
        value = (grads[0, z, here, :].astype(f32) + change).astype(bf16)
        in_grads_ref[here, :] = value
        for w in (0, 1):
            source = in_grads_ref.at[here, pl.ds(w * wide, wide)]
            live["g", s, w] = (
                go(source, gather.at[s, w, 0], up[w]),
                go(source, gather.at[s, w, 2], down[w]),
            )

    lower, upper = pl.ds(0, narrow), pl.ds(narrow, narrow)

    def relay(s, w):
        one, three = live["g", s, w]
        one.wait_recv()
        a = go(gather.at[s, w, 0, all_rows, lower], gather.at[s, w, 1, all_rows, lower], up[w])
        three.wait_recv()
        b = go(gather.at[s, w, 2, all_rows, upper], gather.at[s, w, 1, all_rows, upper], down[w])
        live["r", s, w] = (a, b)

    def sums(s, w):
        for c in live["r", s, w]:
            c.wait_recv()

        def body(i, carry):
            cols = pl.ds(pl.multiple_of(i * 256, 256), 256)
            own = pl.ds(pl.multiple_of(w * wide + i * 256, 256), 256)
            blocks = [in_grads_ref[pl.ds(s * SLAB, SLAB), own].astype(f32)]
            blocks += [gather[s, w, t, :, cols].astype(f32) for t in range(3)]
            for r in range(4):
                total = blocks[0] * coeffs[w, r, 0]
                for t in (1, 2, 3):
                    total = total + blocks[t] * coeffs[w, r, t]
                if r == 0:
                    kept[s, w, :, cols] = total
                else:
                    stage[s, w, r - 1, :, cols] = total.astype(bf16)
            return carry

        lax.fori_loop(0, wide // 256, body, 0)
        u, d = up[1 - w], down[1 - w]
        live["p", s, w] = (
            go(stage.at[s, w, 1, all_rows, lower], arrived.at[s, w, 2, all_rows, lower], u),
            go(stage.at[s, w, 1, all_rows, upper], arrived.at[s, w, 2, all_rows, upper], d),
        )
        live["q", s, w] = [
            go(stage.at[s, w, 0, all_rows, upper], arrived.at[s, w, 0, all_rows, upper], u),
            go(stage.at[s, w, 2, all_rows, lower], arrived.at[s, w, 1, all_rows, lower], d),
        ]

    def late(s, w):
        a, b = live["p", s, w]
        u, d = up[1 - w], down[1 - w]
        a.wait_recv()
        plus(stage.at[s, w, 0, all_rows, lower], arrived.at[s, w, 2, all_rows, lower])
        live["q", s, w].append(
            go(stage.at[s, w, 0, all_rows, lower], arrived.at[s, w, 0, all_rows, lower], u)
        )
        b.wait_recv()
        plus(stage.at[s, w, 2, all_rows, upper], arrived.at[s, w, 2, all_rows, upper])
        live["q", s, w].append(
            go(stage.at[s, w, 2, all_rows, upper], arrived.at[s, w, 1, all_rows, upper], d)
        )

    def finish(s):
        here = pl.ds(s * SLAB, SLAB)
        for w in (1, 0):
            for c in live["q", s, w]:
                c.wait_recv()
            cols = pl.ds(w * wide, wide)
            total = pending[here, cols].astype(f32) + kept[s, w]
            total = total + arrived[s, w, 0].astype(f32) + arrived[s, w, 1].astype(f32)
            updated_ref[here, cols] = total.astype(bf16)

    stages = {
        "product": product, "producta": first_half, "productb": lambda s: product(s, 3),
        "first": lambda s: first(s, whole), "firsta": lambda s: first(s, early),
        "firstb": lambda s: first(s, latter), "second": second, "across": cross, "norm": norm_back,
        "relay_y": lambda s: relay(s, 0), "relay_z": lambda s: relay(s, 1),
        "sums_y": lambda s: sums(s, 0), "sums_z": lambda s: sums(s, 1),
        "late_y": lambda s: late(s, 0), "late_z": lambda s: late(s, 1), "finish": finish,
    }
    own_half()
    for c in swaps:
        c.wait_recv()
    def settle(keep):
        while len(sends) > keep:
            sends.pop(0).wait_send()

    for name in SUMS:
        if name[:-1] in ("second", "norm", "finish"):
            settle(30)
        stages[name[:-1]](int(name[-1]))
    settle(0)


def on_device(saved_in, out_grad, pending, gain, alpha, w_query, w_key, w_value, w_out):
    _, rows, depth = saved_in.shape
    width = w_query.shape[2]
    tokens = 16 * rows
    slabs = rows // SLAB
    wide = depth // 2
    vmem = pl.BlockSpec(memory_space=pltpu.VMEM)
    hbm = pl.BlockSpec(memory_space=pltpu.HBM)
    rows_out = pltpu.VMEM((rows, depth), bf16)

    def buffer(*shape):
        return pltpu.VMEM(shape, bf16)

    grad_input, updated = pl.pallas_call(
        kernel,
        out_shape=(rows_out, rows_out),
        in_specs=[hbm] * 9,
        out_specs=(vmem, vmem),
        scratch_shapes=[
            pltpu.SMEM(alpha.shape, f32),
            buffer(rows, depth),
            pltpu.VMEM((1, depth), f32),
            buffer(4, 2, rows, depth),
            buffer(4, 2, rows, depth),
            buffer(2, 3, depth, width),
            buffer(2, width, depth),
            buffer(4, tokens // 2, width),
            buffer(2, 4, tokens // 2, width),
            buffer(tokens, width),
            buffer(tokens, width),
            buffer(tokens, width),
            buffer(tokens, width),
            pltpu.VMEM((width // HEAD, tokens, tokens), f32),
            pltpu.VMEM((width // HEAD, HEAD, tokens), f32),
            pltpu.VMEM((tokens, HEAD), f32),
            pltpu.VMEM((tokens, HEAD), f32),
            pltpu.VMEM((3, 4 * rows, 512), f32),
            buffer(2, 3, tokens // 2, width),
            buffer(3, tokens // 2, width),
            buffer(slabs, 4, 2, SLAB, depth),
            buffer(slabs, 2, SLAB, depth),
            buffer(slabs, 2, 2, SLAB, depth),
            buffer(4, SLAB, depth),
            buffer(slabs, SLAB, depth),
            buffer(rows, depth),
            buffer(slabs, 2, 3, SLAB, wide),
            buffer(slabs, 2, 3, SLAB, wide),
            buffer(slabs, 2, 3, SLAB, wide),
            pltpu.VMEM((slabs, 2, SLAB, wide), f32),
            pltpu.SemaphoreType.DMA((48 + 28 * slabs,)),
            pltpu.SemaphoreType.DMA((48 + 28 * slabs,)),
            pltpu.SemaphoreType.DMA((9,)),
        ],
        compiler_params=pltpu.CompilerParams(
            collective_id=1, has_side_effects=True, vmem_limit_bytes=59 * 2**20
        ),
        cost_estimate=pl.CostEstimate(flops=14 * 10**9, bytes_accessed=10**7, transcendentals=10**6),
    )(*(pltpu.with_memory_space_constraint(a, pltpu.HBM) for a in (
        alpha, saved_in[0], gain, out_grad[0], pending[0], w_query[0], w_key[0], w_value[0], w_out[0])))
    return (grad_input[None], updated[None])


def solution(mesh):
    return jax.shard_map(
        on_device,
        mesh=mesh,
        in_specs=(
            P("section", "tp", None),
            P("section", "tp", None),
            P("section", "tp", None),
            P("section", None),
            P(),
            P("section", None, "tp"),
            P("section", None, "tp"),
            P("section", None, "tp"),
            P("section", "tp", None),
        ),
        out_specs=(P("section", "tp", None), P("section", "tp", None)),
        check_vma=False,
    )
```

```python
import math

import jax
import jax.numpy as jnp
from jax import lax
from jax.experimental import pallas as pl
from jax.experimental.pallas import tpu as pltpu
from jax.sharding import PartitionSpec as P

HEAD = 128
SLAB = 16
MESH = pl.DeviceIdType.MESH

eps = 1e-05

f32, bf16 = jnp.float32, jnp.bfloat16

GATHER = (
    "gLlo", "gRlo", "gA", "nrm", "nRhi", "gLhi", "nLlo", "gxR", "nLhi", "nA", "nRlo", "gxL", "gRhi",
    "g3A", "oRlo", "oLhi", "P0t", "P0", "oRhi", "oLlo", "g1A", "G0", "G3", "oxL", "nxR", "oxR",
    "P1t", "g2Ahi", "P3t", "nxL", "P3", "P1", "g2Alo", "G1", "zxR", "zxL", "P2t", "P2", "S", "G2",
)
SUMS = (
    "producta0", "firsta1", "firsta0", "productb0", "firstb0", "firstb1", "product2", "second1",
    "across1", "second0", "across0", "norm1", "first2", "norm0", "relay_z1", "relay_y1", "first3",
    "relay_y0", "sums_y1", "second2", "relay_z0", "sums_z1", "sums_y0", "second3", "across2",
    "sums_z0", "late_z1", "across3", "norm2", "late_z0", "norm3", "relay_z2", "relay_y3",
    "relay_y2", "late_y1", "relay_z3", "sums_y3", "sums_z2", "sums_y2", "sums_z3", "finish1",
    "late_y3", "late_y0", "late_z2", "late_y2", "late_z3", "finish0", "finish3", "finish2",
)
ACROSS_FIRST = (0,)


def dot(a, b, ca, cb):
    return lax.dot_general(a, b, (((ca,), (cb,)), ((), ())), preferred_element_type=f32)


def neighbours():
    place = lax.axis_index("tp")
    x, z, core = place // 4, lax.rem(place // 2, 2), lax.rem(place, 2)
    right = lax.rem(x + 1, 4) * 4 + z * 2 + core
    left = lax.rem(x + 3, 4) * 4 + z * 2 + core
    across = x * 4 + (1 - z) * 2 + core
    twin = x * 4 + z * 2 + (1 - core)
    return x, z, core, {"tp": right}, {"tp": left}, {"tp": across}, {"tp": twin}


def kernel(alpha_in, saved_in, gain_in, grad_ref, pending_ref, wq_ref, wk_ref, wv_ref, wo_ref,
           in_grads_ref, updated_ref,
           alpha_ref, saved_ref, gain_ref, normed, grads, weights, out_weights, theirs, heads,
           q_ref, k_ref, v_ref, g_ref, probs_f, outputs, dk_acc, dv_acc, own_sums,
           back, back_twin, part, xb1, xb2, za, zb,
           pending, gather, stage, arrived, kept,
           send_sem, recv_sem, load_sem):
    x, z, core, right, left, across, twin = neighbours()
    section = lax.axis_index("section")
    y, zh = section // 4, lax.rem(section, 4)
    rows, depth = saved_ref.shape
    width = wq_ref.shape[1]
    pair, half = 2 * rows, rows // 2
    wide = depth // 2
    narrow = wide // 2
    other = 1 - z

    def at(dy, dz):
        return lax.rem(y + dy + 4, 4) * 4 + lax.rem(zh + dz + 4, 4)

    up = ({"section": at(1, 0)}, {"section": at(0, 1)})
    down = ({"section": at(3, 0)}, {"section": at(0, 3)})

    sends, indices, local = [], iter(range(send_sem.shape[0])), iter(range(load_sem.shape[0]))

    def go(src, dst, to):
        index = next(indices)
        c = pltpu.make_async_remote_copy(
            src_ref=src, dst_ref=dst, send_sem=send_sem.at[index], recv_sem=recv_sem.at[index],
            device_id=to, device_id_type=MESH,
        )
        c.start()
        sends.append(c)
        return c

    def move(src, dst):
        c = pltpu.make_async_copy(src, dst, load_sem.at[next(local)])
        c.start()
        return c

    load_rows = [move(saved_in, saved_ref), move(gain_in, gain_ref)]
    own_grads = move(grad_ref, grads.at[0, z])
    loads = [
        move(wq_ref, weights.at[0, 0]),
        move(wk_ref, weights.at[0, 1]),
        move(wv_ref, weights.at[0, 2]),
        move(wo_ref, out_weights.at[0]),
    ]
    load_late = [move(pending_ref, pending), move(alpha_in, alpha_ref)]

    barrier = pltpu.get_barrier_semaphore()
    friends = (right, left, across, twin) + up + down
    for friend in friends:
        pl.semaphore_signal(barrier, inc=1, device_id=friend, device_id_type=MESH)
    for c in load_rows:
        c.wait()

    def one(i, carry):
        here = pl.ds(pl.multiple_of(i * 16, 16), 16)
        values = saved_ref[here, :].astype(f32)
        factor = lax.rsqrt(jnp.mean(values * values, axis=-1, keepdims=True) + eps)
        normed[0, z, here, :] = (values * factor * gain_ref[...]).astype(bf16)
        return carry

    lax.fori_loop(0, rows // 16, one, 0)
    pl.semaphore_wait(barrier, len(friends))

    w_twin = []
    lo, hi = pl.ds(0, half), pl.ds(half, half)
    quarter = [pl.ds(i * SLAB, SLAB) for i in range(rows // SLAB)]
    sent = {}

    def trade_weights():
        for j, w in enumerate((wq_ref, wk_ref, wv_ref)):
            w_twin.append(go(w, weights.at[1, j], twin))
        w_twin.append(go(wo_ref, out_weights.at[1], twin))

    def place_of(r):
        return pl.ds(pl.multiple_of(lax.rem(x + 4 - r, 4) * pair, pair), pair)

    results = []

    def hand_over(r, first, count):
        js, here = pl.ds(first, count), place_of(r)
        results.append(go(theirs.at[js, here], heads.at[core, js, here], twin))

    def project(r, which):
        if r == 0:
            for c in (w_twin if which else loads)[:3]:
                c.wait_recv() if which else c.wait()
        here = place_of(r)

        def one(j, carry):
            product = dot(normed[r].reshape(pair, depth), weights[which, j], 1, 0).astype(bf16)
            if which == 0:
                heads[core, j, here, :] = product
            else:
                theirs[j, here, :] = product
            return carry

        lax.fori_loop(0, 3, one, 0)
        if which == 1:
            hand_over(r, 0, 3)

    def project_grads(r):
        if r == 0:
            own_grads.wait()
            loads[3].wait()
            w_twin[3].wait_recv()
        here = place_of(r)
        for which in (1, 0):
            product = dot(grads[r].reshape(pair, depth), out_weights[which], 1, 1).astype(bf16)
            if which == 0:
                heads[core, 3, here, :] = product
            else:
                theirs[3, here, :] = product
                hand_over(r, 3, 1)

    mine, crossed = normed.at[0, z], normed.at[0, other]
    moves = {
        "gA": ((), grad_ref, grads.at[0, z], across),
        "nA": ((), mine, mine, across),
        "gxR": (("gRlo",), grads.at[1, z, lo], grads.at[2, z, lo], right),
        "gxL": (("gLhi",), grads.at[3, z, hi], grads.at[2, z, hi], left),
        "nxR": (("nRlo",), normed.at[1, z, lo], normed.at[2, z, lo], right),
        "nxL": (("nLhi",), normed.at[3, z, hi], normed.at[2, z, hi], left),
        "oxR": (("oRlo",), normed.at[1, other, lo], normed.at[2, other, lo], right),
        "oxL": (("oLhi",), normed.at[3, other, hi], normed.at[2, other, hi], left),
        "g1A": (("gRlo", "gRhi"), grads.at[1, z], grads.at[1, z], across),
        "g3A": (("gLlo", "gLhi"), grads.at[3, z], grads.at[3, z], across),
        "g2Alo": (("gxR",), grads.at[2, z, quarter[1]], grads.at[2, z, quarter[1]], across),
        "g2Ahi": (("gxL",), grads.at[2, z, quarter[2]], grads.at[2, z, quarter[2]], across),
        "zxR": (("g1A",), grads.at[1, other, quarter[0]], grads.at[2, other, quarter[0]], right),
        "zxL": (("g3A",), grads.at[3, other, quarter[3]], grads.at[2, other, quarter[3]], left),
    }
    for end, part_rows in (("lo", lo), ("hi", hi)):
        for way, r, to in (("R", 1, right), ("L", 3, left)):
            moves["g" + way + end] = ((), grad_ref.at[part_rows], grads.at[r, z, part_rows], to)
            moves["n" + way + end] = ((), mine.at[part_rows], normed.at[r, z, part_rows], to)
            moves["o" + way + end] = (("nA",), crossed.at[part_rows], normed.at[r, other, part_rows], to)
    needs = {
        "P0": ("nA",), "P1": ("nRlo", "nRhi", "oRlo", "oRhi"), "P3": ("nLlo", "nLhi", "oLlo", "oLhi"),
        "P2": ("nxR", "nxL", "oxR", "oxL"), "G0": ("gA",), "G1": ("gRlo", "gRhi", "g1A"),
        "G3": ("gLlo", "gLhi", "g3A"), "G2": ("gxR", "gxL", "g2Alo", "g2Ahi", "zxR", "zxL"),
    }
    tokens = q_ref.shape[0]
    block = 512
    chips = tokens // pair
    scale = 1.0 / math.sqrt(HEAD)
    places = [(chip, c) for chip in range(chips) for c in (0, 1)]
    below = lax.broadcasted_iota(jnp.int32, (block, block), 0) <= lax.broadcasted_iota(
        jnp.int32, (block, block), 1
    )

    def assemble(j, ref):
        for chip, c in places:
            ref[pl.ds((2 * chip + c) * rows, rows), :] = heads[c, j, pl.ds(chip * rows, rows), :]

    def take_scores():
        for c in results:
            c.wait_recv()
        results.clear()
        for j, ref in enumerate((q_ref, k_ref, v_ref)):
            assemble(j, ref)
        for head in range(width // HEAD):
            cols = pl.ds(head * HEAD, HEAD)
            values_t = v_ref[:, cols].T
            for step in reversed(range(tokens // block)):
                n = (step + 1) * block
                mine_rows = pl.ds(step * block, block)
                scores = dot(k_ref[pl.ds(0, n), cols], q_ref[mine_rows, cols], 1, 1)
                scores = scores * (scale * math.log2(math.e))
                last = jnp.where(below, scores[n - block :], -1e30)
                scores = last if step == 0 else jnp.concatenate((scores[: n - block], last), axis=0)
                exps = jnp.exp2(scores - jnp.max(scores, axis=0, keepdims=True))
                exps = exps * (1.0 / jnp.sum(exps, axis=0, keepdims=True))
                probs_f[head, pl.ds(0, n), mine_rows] = exps
                outputs[head, :, mine_rows] = dot(values_t[:, :n], exps.astype(bf16), 1, 0)

    landed = set()

    def need(names):
        for name in names:
            if name not in landed:
                landed.add(name)
                sent[name].wait_recv()

    for name in GATHER:
        if name == "nrm":
            trade_weights()
        elif name == "S":
            take_scores()
        elif name in moves:
            waits, src, dst, to = moves[name]
            need(waits)
            sent[name] = go(src, dst, to)
        else:
            need(needs[name[:2]])
            if name[0] == "P":
                project(int(name[1]), 1 if name.endswith("t") else 0)
            else:
                project_grads(int(name[1]))
    for c in results:
        c.wait_recv()

    assemble(3, g_ref)

    def put(j, chip, c, cols, value):
        for s in range(rows // SLAB):
            there = pl.ds((s * chips + chip) * SLAB, SLAB)
            back[c, j, there, cols] = value[s * SLAB : (s + 1) * SLAB].astype(bf16)

    swaps = []
    for head in range(width // HEAD):
        cols = pl.ds(head * HEAD, HEAD)
        keys_t = k_ref[:, cols].T
        for step in reversed(range(tokens // block)):
            n = (step + 1) * block
            mine_rows = pl.ds(step * block, block)
            query, grad = q_ref[mine_rows, cols], g_ref[mine_rows, cols]
            delta = jnp.sum(grad.astype(f32).T * outputs[head, :, mine_rows], axis=0, keepdims=True)
            grad_probs = dot(v_ref[pl.ds(0, n), cols], grad, 1, 1)
            exps = probs_f[head, pl.ds(0, n), mine_rows]
            grad_scores = (exps * ((grad_probs - delta) * scale)).astype(bf16)
            grad_query = dot(keys_t[:, :n], grad_scores, 1, 0).T
            for chip, c in places:
                offset = (2 * chip + c) * rows - step * block
                if 0 <= offset < block:
                    put(0, chip, c, cols, grad_query[offset : offset + rows])
            more_k = dot(grad_scores, query, 1, 0)
            more_v = dot(exps.astype(bf16), grad, 1, 0)
            if step == tokens // block - 1:
                dk_acc[...] = more_k
                dv_acc[...] = more_v
            else:
                dk_acc[pl.ds(0, n)] += more_k
                dv_acc[pl.ds(0, n)] += more_v
        for j, acc in ((1, dk_acc), (2, dv_acc)):
            for chip, c in places:
                put(j, chip, c, cols, acc[pl.ds((2 * chip + c) * rows, rows), :])
        everything = pl.ds(0, tokens // 2)
        swaps.append(go(back.at[1 - core, :, everything, cols], back_twin.at[:, everything, cols], twin))

    slabs = rows // SLAB
    all_rows = pl.ds(0, SLAB)
    chunk = 512
    together = chips * SLAB

    def coefficient(j, s):
        return jnp.where(s > j, alpha_ref[s, j], 0.0)

    for c in load_late:
        c.wait()
    coeffs = {}
    for r in range(4):
        for t in range(4):
            coeffs[0, r, t] = coefficient(at(0, r), at(4 - t, 0))
            coeffs[1, r, t] = coefficient(at(r, 0), at(0, 4 - t))

    def spot(r):
        return lax.rem(x + r, 4)

    def plus(target, source):
        target[...] = (target[...].astype(f32) + source[...].astype(f32)).astype(bf16)

    live = {}

    def partial(j, s, n, lefts):
        here = pl.ds(s * together, 2 * together)
        cols = pl.ds(pl.multiple_of(n * chunk, chunk), chunk)
        total = dot(lefts[0, here, :], weights[j, 0, cols, :], 1, 1)
        for k in (1, 2):
            total += dot(lefts[k, here, :], weights[j, k, cols, :], 1, 1)
        return total

    def store(s, n, total):
        cols = pl.ds(pl.multiple_of(n * chunk, chunk), chunk)
        part[s : s + 2, :, :, :, cols] = total.astype(bf16).reshape(2, chips // 2, 2, SLAB, chunk)

    def product(s, begin=0):
        def step(n, carry):
            store(s, n, partial(0, s, n, back.at[core]) + partial(1, s, n, back_twin))
            return carry

        lax.fori_loop(begin, depth // chunk, step, 0)

    def own_half():
        def step(n, carry):
            own_sums[n] = partial(0, 0, n, back.at[core])
            return carry

        lax.fori_loop(0, 3, step, 0)

    def first_half(s):
        def step(n, carry):
            store(s, n, own_sums[n] + partial(1, s, n, back_twin))
            return carry

        lax.fori_loop(0, 3, step, 0)

    early, latter = pl.ds(0, wide), pl.ds(wide, wide)

    whole = pl.ds(0, depth)

    def first(s, cols):
        def lay(key, src, dst, to):
            live.setdefault(key, []).append(go(src.at[all_rows, cols], dst.at[all_rows, cols], to))

        if s in ACROSS_FIRST:
            for r in (2, 1, 3, 0):
                lay(("za", s, r), part.at[s, spot(r), other], za.at[r], across)
            return
        lay(("x1r", s), part.at[s, spot(2), 0], xb1.at[s, 0], right)
        lay(("x1l", s), part.at[s, spot(2), 1], xb1.at[s, 1], left)
        lay(("x2", s), part.at[s, spot(1), 1], xb2.at[s, 0, 1], right)
        lay(("x2", s), part.at[s, spot(3), 0], xb2.at[s, 1, 0], left)

    def arrive(*key):
        for c in live[key]:
            c.wait_recv()

    def second(s):
        if s in ACROSS_FIRST:
            two, one, three = (part.at[s, spot(r), z] for r in (2, 1, 3))
            arrive("za", s, 2)
            plus(two, za.at[2])
            live["x1r", s] = [go(two.at[all_rows, early], xb1.at[s, 0, all_rows, early], right)]
            live["x1l", s] = [go(two.at[all_rows, latter], xb1.at[s, 0, all_rows, latter], left)]
            arrive("za", s, 1)
            plus(one, za.at[1])
            live["x2", s] = [go(one.at[all_rows, latter], xb2.at[s, 0, 0, all_rows, latter], right)]
            arrive("za", s, 3)
            plus(three, za.at[3])
            live["x2", s].append(go(three.at[all_rows, early], xb2.at[s, 1, 0, all_rows, early], left))
            return
        arrive("x1r", s)
        plus(part.at[s, spot(1), 0], xb1.at[s, 0])
        live["x2", s].append(go(part.at[s, spot(1), 0], xb2.at[s, 0, 0], right))
        arrive("x1l", s)
        plus(part.at[s, spot(3), 1], xb1.at[s, 1])
        live["x2", s].append(go(part.at[s, spot(3), 1], xb2.at[s, 1, 1], left))

    def cross(s):
        if s in ACROSS_FIRST:
            one, three = (part.at[s, spot(r), z] for r in (1, 3))
            arrive("x1r", s)
            plus(one.at[all_rows, early], xb1.at[s, 0, all_rows, early])
            live["x2", s].append(go(one.at[all_rows, early], xb2.at[s, 0, 0, all_rows, early], right))
            arrive("x1l", s)
            plus(three.at[all_rows, latter], xb1.at[s, 0, all_rows, latter])
            live["x2", s].append(go(three.at[all_rows, latter], xb2.at[s, 1, 0, all_rows, latter], left))
            return
        for c in live["x2", s]:
            c.wait_recv()
        total = part[s, x, other].astype(f32) + xb2[s, 0, other].astype(f32) + xb2[s, 1, other].astype(f32)
        part[s, x, other] = total.astype(bf16)
        live["z", s] = go(part.at[s, x, other], zb.at[s], across)

    def norm_back(s):
        here = pl.ds(s * SLAB, SLAB)
        if s in ACROSS_FIRST:
            arrive("x2", s)
            arrive("za", s, 0)
        else:
            live["z", s].wait_recv()
        saved = saved_ref[here, :].astype(f32)
        last, k = (za[0], 0) if s in ACROSS_FIRST else (zb[s], z)
        total = part[s, x, z].astype(f32) + xb2[s, 0, k].astype(f32)
        total = total + xb2[s, 1, k].astype(f32) + last.astype(f32)
        factor = lax.rsqrt(jnp.mean(saved * saved, axis=-1, keepdims=True) + eps)
        scaled = total * gain_ref[...]
        inner = jnp.mean(scaled * saved, axis=-1, keepdims=True)
        change = factor * (scaled - saved * (factor * factor * inner))
        value = (grads[0, z, here, :].astype(f32) + change).astype(bf16)
        in_grads_ref[here, :] = value
        for w in (0, 1):
            source = in_grads_ref.at[here, pl.ds(w * wide, wide)]
            live["g", s, w] = (
                go(source, gather.at[s, w, 0], up[w]),
                go(source, gather.at[s, w, 2], down[w]),
            )

    lower, upper = pl.ds(0, narrow), pl.ds(narrow, narrow)

    def relay(s, w):
        one, three = live["g", s, w]
        one.wait_recv()
        a = go(gather.at[s, w, 0, all_rows, lower], gather.at[s, w, 1, all_rows, lower], up[w])
        three.wait_recv()
        b = go(gather.at[s, w, 2, all_rows, upper], gather.at[s, w, 1, all_rows, upper], down[w])
        live["r", s, w] = (a, b)

    def sums(s, w):
        for c in live["r", s, w]:
            c.wait_recv()

        def body(i, carry):
            cols = pl.ds(pl.multiple_of(i * 256, 256), 256)
            own = pl.ds(pl.multiple_of(w * wide + i * 256, 256), 256)
            blocks = [in_grads_ref[pl.ds(s * SLAB, SLAB), own].astype(f32)]
            blocks += [gather[s, w, t, :, cols].astype(f32) for t in range(3)]
            for r in range(4):
                total = blocks[0] * coeffs[w, r, 0]
                for t in (1, 2, 3):
                    total = total + blocks[t] * coeffs[w, r, t]
                if r == 0:
                    kept[s, w, :, cols] = total
                else:
                    stage[s, w, r - 1, :, cols] = total.astype(bf16)
            return carry

        lax.fori_loop(0, wide // 256, body, 0)
        u, d = up[1 - w], down[1 - w]
        live["p", s, w] = (
            go(stage.at[s, w, 1, all_rows, lower], arrived.at[s, w, 2, all_rows, lower], u),
            go(stage.at[s, w, 1, all_rows, upper], arrived.at[s, w, 2, all_rows, upper], d),
        )
        live["q", s, w] = [
            go(stage.at[s, w, 0, all_rows, upper], arrived.at[s, w, 0, all_rows, upper], u),
            go(stage.at[s, w, 2, all_rows, lower], arrived.at[s, w, 1, all_rows, lower], d),
        ]

    def late(s, w):
        a, b = live["p", s, w]
        u, d = up[1 - w], down[1 - w]
        a.wait_recv()
        plus(stage.at[s, w, 0, all_rows, lower], arrived.at[s, w, 2, all_rows, lower])
        live["q", s, w].append(
            go(stage.at[s, w, 0, all_rows, lower], arrived.at[s, w, 0, all_rows, lower], u)
        )
        b.wait_recv()
        plus(stage.at[s, w, 2, all_rows, upper], arrived.at[s, w, 2, all_rows, upper])
        live["q", s, w].append(
            go(stage.at[s, w, 2, all_rows, upper], arrived.at[s, w, 1, all_rows, upper], d)
        )

    def finish(s):
        here = pl.ds(s * SLAB, SLAB)
        for w in (1, 0):
            for c in live["q", s, w]:
                c.wait_recv()
            cols = pl.ds(w * wide, wide)
            total = pending[here, cols].astype(f32) + kept[s, w]
            total = total + arrived[s, w, 0].astype(f32) + arrived[s, w, 1].astype(f32)
            updated_ref[here, cols] = total.astype(bf16)

    stages = {
        "product": product, "producta": first_half, "productb": lambda s: product(s, 3),
        "first": lambda s: first(s, whole), "firsta": lambda s: first(s, early),
        "firstb": lambda s: first(s, latter), "second": second, "across": cross, "norm": norm_back,
        "relay_y": lambda s: relay(s, 0), "relay_z": lambda s: relay(s, 1),
        "sums_y": lambda s: sums(s, 0), "sums_z": lambda s: sums(s, 1),
        "late_y": lambda s: late(s, 0), "late_z": lambda s: late(s, 1), "finish": finish,
    }
    own_half()
    for c in swaps:
        c.wait_recv()
    def settle(keep):
        while len(sends) > keep:
            sends.pop(0).wait_send()

    for name in SUMS:
        if name[:-1] in ("second", "norm", "finish"):
            settle(30)
        stages[name[:-1]](int(name[-1]))
    settle(0)


def on_device(saved_in, out_grad, pending, gain, alpha, w_query, w_key, w_value, w_out):
    _, rows, depth = saved_in.shape
    width = w_query.shape[2]
    tokens = 16 * rows
    slabs = rows // SLAB
    wide = depth // 2
    vmem = pl.BlockSpec(memory_space=pltpu.VMEM)
    hbm = pl.BlockSpec(memory_space=pltpu.HBM)
    rows_out = pltpu.VMEM((rows, depth), bf16)

    def buffer(*shape):
        return pltpu.VMEM(shape, bf16)

    grad_input, updated = pl.pallas_call(
        kernel,
        out_shape=(rows_out, rows_out),
        in_specs=[hbm] * 9,
        out_specs=(vmem, vmem),
        scratch_shapes=[
            pltpu.SMEM(alpha.shape, f32),
            buffer(rows, depth),
            pltpu.VMEM((1, depth), f32),
            buffer(4, 2, rows, depth),
            buffer(4, 2, rows, depth),
            buffer(2, 3, depth, width),
            buffer(2, width, depth),
            buffer(4, tokens // 2, width),
            buffer(2, 4, tokens // 2, width),
            buffer(tokens, width),
            buffer(tokens, width),
            buffer(tokens, width),
            buffer(tokens, width),
            pltpu.VMEM((width // HEAD, tokens, tokens), f32),
            pltpu.VMEM((width // HEAD, HEAD, tokens), f32),
            pltpu.VMEM((tokens, HEAD), f32),
            pltpu.VMEM((tokens, HEAD), f32),
            pltpu.VMEM((3, 4 * rows, 512), f32),
            buffer(2, 3, tokens // 2, width),
            buffer(3, tokens // 2, width),
            buffer(slabs, 4, 2, SLAB, depth),
            buffer(slabs, 2, SLAB, depth),
            buffer(slabs, 2, 2, SLAB, depth),
            buffer(4, SLAB, depth),
            buffer(slabs, SLAB, depth),
            buffer(rows, depth),
            buffer(slabs, 2, 3, SLAB, wide),
            buffer(slabs, 2, 3, SLAB, wide),
            buffer(slabs, 2, 3, SLAB, wide),
            pltpu.VMEM((slabs, 2, SLAB, wide), f32),
            pltpu.SemaphoreType.DMA((48 + 28 * slabs,)),
            pltpu.SemaphoreType.DMA((48 + 28 * slabs,)),
            pltpu.SemaphoreType.DMA((9,)),
        ],
        compiler_params=pltpu.CompilerParams(
            collective_id=1, has_side_effects=True, vmem_limit_bytes=59 * 2**20
        ),
        cost_estimate=pl.CostEstimate(flops=14 * 10**9, bytes_accessed=10**7, transcendentals=10**6),
    )(*(pltpu.with_memory_space_constraint(a, pltpu.HBM) for a in (
        alpha, saved_in[0], gain, out_grad[0], pending[0], w_query[0], w_key[0], w_value[0], w_out[0])))
    return (grad_input[None], updated[None])


def solution(mesh):
    return jax.shard_map(
        on_device,
        mesh=mesh,
        in_specs=(
            P("section", "tp", None),
            P("section", "tp", None),
            P("section", "tp", None),
            P("section", None),
            P(),
            P("section", None, "tp"),
            P("section", None, "tp"),
            P("section", None, "tp"),
            P("section", "tp", None),
        ),
        out_specs=(P("section", "tp", None), P("section", "tp", None)),
        check_vma=False,
    )
```
